32 devices in a mesh: ctx: 16 (over z, y, core), head: 2 (over x).
Axes of the slice: x: 2, y: 2, z: 4, core: 2. Of those that a mesh axis runs over, the one named last changes fastest.
Arguments:
- queries: bfloat16 [8192, 4096], P(('ctx', 'head')), may hold values from -12 to 12
- keys: bfloat16 [8192, 1024], P(('ctx', 'head')), may hold values from -12 to 12
- values: bfloat16 [8192, 1024], P(('ctx', 'head')), may hold values from -6 to 6
- doc_lengths: int32 [4], replicated, may hold values from 1 to 4096, 8192 in all
- piece_owner: int32 [16, 16], P('ctx'), may hold values from 0 to 15, each once within a row
Outputs:
- owned: bfloat16 [8192, 4096], P('ctx', 'head')
The draws below stay inside these ranges and needn't reach their ends.
Inputs may be any that keep to these rules, and one draw needn't show every extreme that they name: Each row of piece_owner is a permutation of 0 .. 15. doc_lengths sum to 8192, and the largest equals 4096.
All inputs are finite; a program needn't handle non-finite values.
Results may differ from the reference program's by a relative error of at most 0.0033.
Values may be sent and summed in bfloat16 or wider, within the bound.
No kernel may reach another device: no remote copies, remote signals or barrier semaphores. Data moves between devices by JAX's collectives and lax.ppermute only.
A program may use at most 128 MiB of HBM per device.

```python
import math
import jax
import jax.numpy as jnp
import numpy as np
from jax import lax

HD = 128
KVH = 8
QPK = 4
QH = 32
TOK_DEV = 512
MOST = 4096
SEQ = 8192
NDOC = 4
REACH = 8
PIECE = 32
N_CTX = 16


def draw_queries(key, part):
    drawn = 1.5 * jnp.clip(jax.random.normal(jax.random.fold_in(key, 11), (SEQ, QH * HD)), -6.0, 6.0)
    return drawn.astype(jnp.bfloat16)


def draw_keys(key, part):
    drawn = 1.33 * jnp.clip(jax.random.normal(jax.random.fold_in(key, 23), (SEQ, KVH * HD)), -6.0, 6.0)
    return drawn.astype(jnp.bfloat16)


def block_levels(stream_key, shape, shards, low, high):
    def one(position, shards_of):
        steps = jax.random.uniform(jax.random.fold_in(jax.random.fold_in(stream_key, 6), position), (shards_of,), jnp.float32, low / len(shards), high / len(shards))
        return jnp.repeat(jnp.exp(steps), shape[position] // shards_of).reshape((-1,) + (1,) * (len(shape) - position - 1))

    gain = one(*shards[0])
    for cut in shards[1:]:
        gain = gain * one(*cut)
    return gain


def profile(number_of, total, reach, slope):
    portions = [(1 << 20) // math.isqrt(grade ** slope) + 1 for grade in range(2, number_of + 1)]
    rest, holding = total - reach - (number_of - 1), [1] * (number_of - 1)
    while rest > 0:
        candidates = [i for i in range(number_of - 1) if holding[i] < reach]
        whole, budget = sum([portions[i] for i in candidates]), rest
        for i in candidates:
            extra = min(reach - holding[i], max(1, budget * portions[i] // whole), rest)
            holding[i] = holding[i] + extra
            rest = rest - extra
    return np.array([reach] + holding)


def uneven_parts(own_key, number_of, total, reach, skew):
    if number_of == 2:
        one = jax.random.randint(own_key, (), max(1, total - reach), min(reach, total - 1) + 1)
        return jnp.stack([one, total - one])
    lengths = jnp.asarray(profile(number_of, total, reach, skew), jnp.int32)
    couples = (number_of - 1) // 2
    donor, receiver = lengths[1:1 + 2 * couples:2], lengths[2:2 + 2 * couples:2]
    slack = jnp.minimum(donor - 1, reach - receiver)
    passed = jax.random.randint(jax.random.fold_in(own_key, 1), (couples,), 0, 1 << 20) % (slack + 1)
    lengths = lengths.at[1:1 + 2 * couples:2].set(donor - passed).at[2:2 + 2 * couples:2].set(receiver + passed)
    return lengths[jax.random.permutation(jax.random.fold_in(own_key, 2), number_of)]


def normal_values(own_key, dims, scale, limit, cuts=(), held_as=jnp.bfloat16):
    gain = block_levels(own_key, dims, cuts, -0.22, 0.18) if cuts else 1.0
    values = jax.random.normal(own_key, dims, jnp.float32) * scale * gain
    return jnp.minimum(jnp.maximum(values, -limit), limit).astype(held_as)


def setup_inputs(seed: int = 0) -> dict:
    arg_keys = jax.random.split(jax.random.key(seed), 6)
    return {
        "queries": draw_queries(jax.random.fold_in(arg_keys[5], 71), 0),
        "keys": draw_keys(jax.random.fold_in(arg_keys[5], 71), 0),
        "values": normal_values(arg_keys[2], (SEQ, KVH * HD), 1.0, 6.0, ((0, 32),)),
        "doc_lengths": uneven_parts(arg_keys[3], NDOC, SEQ, MOST, 2).astype(jnp.int32),
        "piece_owner": jax.vmap(lambda own: jax.random.permutation(own, N_CTX))(jax.random.split(arg_keys[4], N_CTX)).reshape((N_CTX, N_CTX)).astype(jnp.int32),
    }


masked_score = -1e+30

def doc_index(positions, doc_lengths):
    doc_ends = jnp.cumsum(doc_lengths).astype(jnp.int32)
    return lax.optimization_barrier(jnp.sum((positions[:, None] >= doc_ends[None, :]).astype(jnp.int32), axis=1)).astype(jnp.int32)

def reference(queries, keys, values, doc_lengths, piece_owner):
    window_rows = (REACH + 1) * TOK_DEV
    pad_rows = REACH * TOK_DEV
    score_scale = 1.0 / math.sqrt(HD)
    positions = jnp.arange(SEQ, dtype=jnp.int32)
    doc_ids = doc_index(positions, doc_lengths)
    keys_padded = jnp.concatenate([jnp.zeros((pad_rows, KVH * HD), keys.dtype), keys], axis=0)
    values_padded = jnp.concatenate([jnp.zeros((pad_rows, KVH * HD), values.dtype), values], axis=0)
    ids_padded = jnp.concatenate([jnp.full((pad_rows,), -1, jnp.int32), doc_ids], axis=0)

    def one_block(block_index):
        block_start = (block_index * TOK_DEV).astype(jnp.int32)
        query_block = lax.dynamic_slice_in_dim(queries, block_start, TOK_DEV, 0).astype(jnp.float32).reshape(TOK_DEV, KVH, QPK, HD)
        key_block = lax.dynamic_slice_in_dim(keys_padded, block_start, window_rows, 0).astype(jnp.float32).reshape(window_rows, KVH, HD)
        value_block = lax.dynamic_slice_in_dim(values_padded, block_start, window_rows, 0).astype(jnp.float32).reshape(window_rows, KVH, HD)
        query_position = block_start + jnp.arange(TOK_DEV, dtype=jnp.int32)
        key_position = block_start - pad_rows + jnp.arange(window_rows, dtype=jnp.int32)
        query_ids = lax.dynamic_slice_in_dim(doc_ids, block_start, TOK_DEV, 0)
        key_ids = lax.dynamic_slice_in_dim(ids_padded, block_start, window_rows, 0)
        live_pairs = (key_position[None, :] >= 0) & (key_position[None, :] <= query_position[:, None]) & (key_ids[None, :] == query_ids[:, None])
        live_mask = live_pairs[:, None, None, :]
        scores = jnp.einsum('qgjd,kgd->qgjk', query_block, key_block) * score_scale
        scores = jnp.where(live_mask, scores, masked_score)
        row_top = lax.optimization_barrier(jnp.max(scores, axis=-1, keepdims=True))
        weights = jnp.where(live_mask, jnp.exp(scores - row_top), 0.0)
        row_total = lax.optimization_barrier(jnp.sum(weights, axis=-1))
        rounded = lax.optimization_barrier(weights.astype(jnp.bfloat16)).astype(jnp.float32)
        weighted = jnp.einsum('qgjk,kgd->qgjd', rounded, value_block)
        result = weighted / row_total[..., None]
        return result.reshape(TOK_DEV, QH * HD).astype(jnp.bfloat16)
    attended = lax.map(one_block, jnp.arange(N_CTX, dtype=jnp.int32)).reshape(SEQ, QH * HD)
    source_rows = jnp.broadcast_to(jnp.arange(N_CTX, dtype=jnp.int32)[:, None], (N_CTX, N_CTX))
    piece_cols = jnp.broadcast_to(jnp.arange(N_CTX, dtype=jnp.int32)[None, :], (N_CTX, N_CTX))
    inverse = jnp.zeros((N_CTX, N_CTX), jnp.int32).at[source_rows, piece_owner].set(piece_cols)
    pieces = attended.reshape(N_CTX, N_CTX, PIECE, QH * HD)
    taken = jnp.take_along_axis(pieces, inverse[:, :, None, None], axis=1)
    owned = jnp.transpose(taken, (1, 0, 2, 3)).reshape(SEQ, QH * HD)
    return owned
```

```python
import functools
import math

import jax
import jax.numpy as jnp
from jax import lax
from jax.experimental import pallas as pl
from jax.experimental.pallas import tpu as pltpu
from jax.sharding import Mesh
from jax.sharding import PartitionSpec as P

HD = 128
QPK = 4
MOST = 4096
Q_ROWS = 256
K_ROWS = 512
ONES = 16
MASKED = -1e30
SCALE = math.log2(math.e) / math.sqrt(HD)


def doc_start(place, ends):
    start = jnp.zeros_like(place)
    for end in ends:
        start = jnp.maximum(start, jnp.where(end <= place, end, 0))
    return start


def attend_step(block, masked, base, first_row, ends, qs, ks, vts, top, total):
    rows = pl.ds(pl.multiple_of(block * K_ROWS, K_ROWS), K_ROWS)
    keys = ks[rows, :HD]
    keys = jnp.concatenate([keys, keys], axis=1)
    values = vts[:, rows]
    if masked:
        shape = (K_ROWS, Q_ROWS)
        key_place = base + block * K_ROWS + lax.broadcasted_iota(jnp.int32, shape, 0)
        row = first_row + lax.broadcasted_iota(jnp.int32, (1, Q_ROWS), 1)
        live = (key_place <= row) & (key_place >= doc_start(row, ends))
    for head in range(QPK):
        scores = lax.dot_general(
            keys, qs[head], (((1,), (1,)), ((), ())), preferred_element_type=jnp.float32
        )
        if masked:
            scores = jnp.where(live, scores, MASKED)
        old_top = top[head]
        new_top = jnp.maximum(old_top, jnp.max(scores, axis=0, keepdims=True))
        weights = jnp.exp2(scores - new_top).astype(jnp.bfloat16)
        part = jnp.dot(values, weights, preferred_element_type=jnp.float32)
        total[head] = total[head] * jnp.exp2(old_top - new_top) + part
        top[head] = new_top


def scaled_queries(q_ref, qs):
    for head in range(QPK):
        scaled = q_ref[:, head * HD : (head + 1) * HD].astype(jnp.float32) * SCALE
        high = scaled.astype(jnp.bfloat16)
        qs[head, :, :HD] = high
        qs[head, :, HD:] = (scaled - high.astype(jnp.float32)).astype(jnp.bfloat16)


def turned_values(ks, vts):
    window = ks.shape[0]
    vts[HD:, :] = jnp.ones((ONES, window), jnp.bfloat16)

    def turn(tile, carry):
        rows = pl.ds(pl.multiple_of(tile * HD, HD), HD)
        vts[:HD, rows] = ks[rows, HD:].T
        return carry

    lax.fori_loop(0, window // HD, turn, 0)


def span(low, high, run):
    lax.fori_loop(low, high, lambda block, carry: (run(block), carry)[1], 0)


def near_kernel(info, q_ref, own, near, top_out, total_out, ks, vts, qs, top, total):
    tokens = own.shape[0]
    step = pl.program_id(0)

    @pl.when(step == 0)
    def _():
        ks[:tokens] = near[...]
        ks[tokens:] = own[...]
        turned_values(ks, vts)

    scaled_queries(q_ref, qs)
    top[...] = jnp.full(top.shape, MASKED, jnp.float32)
    total[...] = jnp.zeros(total.shape, jnp.float32)
    ends = [info[1 + doc] for doc in range(info.shape[0] - 1)]
    base = info[0] - tokens
    first_row = info[0] + step * Q_ROWS
    run = functools.partial(
        attend_step, base=base, first_row=first_row, ends=ends, qs=qs, ks=ks, vts=vts, top=top, total=total
    )
    diagonal = (tokens + step * Q_ROWS) // K_ROWS
    first_start = jnp.maximum(doc_start(first_row, ends) - base, 0)
    last_start = jnp.maximum(doc_start(first_row + Q_ROWS - 1, ends) - base, 0)
    whole_from = jnp.minimum((last_start + K_ROWS - 1) // K_ROWS, diagonal)
    run(diagonal, True)
    span(whole_from, diagonal, lambda block: run(block, False))
    span(first_start // K_ROWS, whole_from, lambda block: run(block, True))
    top_out[0] = top[...]
    total_out[0] = total[...]


def far_kernel(info, owner, q_ref, top_in, total_in, *refs):
    far, (out, ks, vts, qs, top, total) = refs[:-6], refs[-6:]
    tokens = far[0].shape[0]
    window = tokens * len(far)
    step = pl.program_id(0)

    ends = [info[1 + doc] for doc in range(info.shape[0] - 1)]
    base = info[0] - tokens - window
    first_row = info[0] + step * Q_ROWS
    first_start = jnp.clip(doc_start(first_row, ends) - base, 0, window)
    last_start = jnp.clip(doc_start(first_row + Q_ROWS - 1, ends) - base, 0, window)

    @pl.when(step == 0)
    def _():
        for index, ref in enumerate(far):
            ks[(len(far) - 1 - index) * tokens : (len(far) - index) * tokens] = ref[...]
        turned_values(ks, vts)

    top[...] = top_in[0]
    total[...] = total_in[0]

    @pl.when(first_start < window)
    def _():
        scaled_queries(q_ref, qs)
        run = functools.partial(
            attend_step, base=base, first_row=first_row, ends=ends, qs=qs, ks=ks, vts=vts, top=top, total=total
        )
        whole_from = (last_start + K_ROWS - 1) // K_ROWS
        span(whole_from, window // K_ROWS, lambda block: run(block, False))
        span(first_start // K_ROWS, whole_from, lambda block: run(block, True))

    piece = out.shape[2]
    for head in range(QPK):
        done = total[head, :HD] / total[head, HD : HD + 1]
        done = done.T.astype(jnp.bfloat16)
        for part in range(Q_ROWS // piece):
            slot = step * (Q_ROWS // piece) + part
            out[owner[slot], slot // out.shape[0], :, head * HD : (head + 1) * HD] = done[
                part * piece : (part + 1) * piece
            ]


def whole_block(shape):
    return pl.BlockSpec(shape, lambda *_: (0,) * len(shape))


def attend(info, owner, n_owner, piece, query_rows, own, steps_back):
    tokens, features = query_rows.shape
    blocks = tokens // Q_ROWS
    near, far = steps_back[0], steps_back[1:]
    query_spec = pl.BlockSpec((Q_ROWS, features), lambda i, *_: (i, 0))
    top_shape = (QPK, 1, Q_ROWS)
    total_shape = (QPK, HD + ONES, Q_ROWS)
    state_specs = [
        pl.BlockSpec((1,) + top_shape, lambda i, *_: (i, 0, 0, 0)),
        pl.BlockSpec((1,) + total_shape, lambda i, *_: (i, 0, 0, 0)),
    ]
    state_shapes = [
        jax.ShapeDtypeStruct((blocks,) + top_shape, jnp.float32),
        jax.ShapeDtypeStruct((blocks,) + total_shape, jnp.float32),
    ]

    def scratch(window):
        return [
            pltpu.VMEM((window, 2 * HD), jnp.bfloat16),
            pltpu.VMEM((HD + ONES, window), jnp.bfloat16),
            pltpu.VMEM((QPK, Q_ROWS, 2 * HD), jnp.bfloat16),
            pltpu.VMEM(top_shape, jnp.float32),
            pltpu.VMEM(total_shape, jnp.float32),
        ]

    params = pltpu.CompilerParams(vmem_limit_bytes=56 * 1024 * 1024)
    state = pl.pallas_call(
        near_kernel,
        grid_spec=pltpu.PrefetchScalarGridSpec(
            num_scalar_prefetch=1,
            grid=(blocks,),
            in_specs=[query_spec, whole_block(own.shape), whole_block(near.shape)],
            out_specs=state_specs,
            scratch_shapes=scratch(2 * tokens),
        ),
        out_shape=state_shapes,
        compiler_params=params,
        cost_estimate=pl.CostEstimate(flops=20_000_000_000, bytes_accessed=1 << 23, transcendentals=0),
        name="attend_near",
    )(info, query_rows, own, near)
    out_shape = (n_owner, tokens // (n_owner * piece), piece, features)
    return pl.pallas_call(
        far_kernel,
        grid_spec=pltpu.PrefetchScalarGridSpec(
            num_scalar_prefetch=2,
            grid=(blocks,),
            in_specs=[query_spec, *state_specs, *(whole_block(ref.shape) for ref in far)],
            out_specs=whole_block(out_shape),
            scratch_shapes=scratch(tokens * len(far)),
        ),
        out_shape=jax.ShapeDtypeStruct(out_shape, jnp.bfloat16),
        compiler_params=params,
        cost_estimate=pl.CostEstimate(flops=5_000_000_000, bytes_accessed=1 << 23, transcendentals=0),
        name="attend_far",
    )(info, owner, query_rows, *state, *far)


def solution(mesh):
    n_ctx, n_head = mesh.shape["ctx"], mesh.shape["head"]

    def run(queries, keys, values, doc_lengths, piece_owner):
        group = keys.shape[1] // (HD * n_head)
        planes = n_ctx // group
        grouped = Mesh(mesh.devices.reshape(planes, group, n_head), ("plane", "local", "head"))
        rows = P(("plane", "local", "head"), None)

        def dealt(array):
            features = array.shape[1] // (n_head * group)
            split = array.reshape(-1, n_head, group, features).transpose(2, 1, 0, 3)
            split = split.reshape(n_head * group, -1, features)
            moved = lax.all_to_all(split, ("local", "head"), split_axis=0, concat_axis=0, tiled=True)
            return moved.reshape(-1, features)

        def per_device(queries, keys, values, doc_lengths, piece_owner):
            heads = n_head * group
            tok = keys.shape[0]
            paired = jnp.concatenate(
                [keys.reshape(tok, heads, HD), values.reshape(tok, heads, HD)], axis=2
            ).reshape(tok, heads * 2 * HD)
            own = dealt(paired)
            tokens = own.shape[0]
            reach = (MOST - 1) // tokens + 1
            up = [(plane, plane + 1) for plane in range(planes - 1)]
            steps_back = []
            moving = own
            for _ in range(reach):
                moving = lax.ppermute(moving, "plane", up)
                steps_back.append(moving)
            query_rows = dealt(queries)
            owner = lax.all_gather(piece_owner, "local", axis=0, tiled=True).reshape(-1)
            start = lax.axis_index("plane") * tokens
            info = jnp.concatenate([start[None], jnp.cumsum(doc_lengths)]).astype(jnp.int32)
            piece = tokens // (group * n_ctx)
            ordered = attend(info, owner, n_ctx, piece, query_rows, own, steps_back)
            received = lax.all_to_all(
                ordered.reshape(n_ctx, group * piece, -1),
                ("plane", "local"),
                split_axis=0,
                concat_axis=0,
                tiled=True,
            )
            features = received.shape[-1]
            received = received.reshape(planes, group, group * piece, features)
            return received.transpose(0, 2, 1, 3).reshape(planes * group * piece, group * features)

        return jax.shard_map(
            per_device,
            mesh=grouped,
            in_specs=(rows, rows, rows, P(), P(("plane", "local"), None)),
            out_specs=P(("plane", "local"), "head"),
            check_vma=False,
        )(queries, keys, values, doc_lengths, piece_owner)

    return run
```

```python
import math

import jax
import jax.numpy as jnp
from jax import lax
from jax.experimental import pallas as pl
from jax.experimental.pallas import tpu as pltpu
from jax.sharding import Mesh
from jax.sharding import PartitionSpec as P

HD = 128
QPK = 4
MOST = 4096
Q_ROWS = 256
K_LONG = 1024
K_SHORT = 256
MASKED = -1e30
SCALE = math.log2(math.e) / math.sqrt(HD)
VMEM = 32 * 1024 * 1024


def doc_start(place, ends):
    start = jnp.zeros_like(place)
    for end in ends:
        start = jnp.maximum(start, jnp.where(end <= place, end, 0))
    return start


class Block:
    def __init__(self, ends, first_row, base, window, turned, values, qs, top, total):
        self.ends = ends
        self.first_row, self.base, self.window = first_row, base, window
        self.turned, self.values, self.qs, self.top, self.total = turned, values, qs, top, total
        self.first_start = doc_start(first_row, self.ends) - base
        self.last_start = doc_start(first_row + Q_ROWS - 1, self.ends) - base

    def load(self, q_ref):
        for head in range(QPK):
            scaled = q_ref[:, head * HD : (head + 1) * HD].astype(jnp.float32) * SCALE
            high = scaled.astype(jnp.bfloat16)
            rows = slice(head * Q_ROWS, (head + 1) * Q_ROWS)
            self.qs[rows, :HD] = high
            self.qs[rows, HD:] = (scaled - high.astype(jnp.float32)).astype(jnp.bfloat16)

    def run(self, at, size, masked):
        at = pl.multiple_of(at, K_SHORT)
        keys = self.turned[:, pl.ds(at, size)]
        keys = jnp.concatenate([keys, keys], axis=0)
        values = self.values[pl.ds(at, size), :]
        values = jnp.concatenate([values, jnp.ones_like(values)], axis=1)
        if masked:
            shape = (Q_ROWS, size)
            row = self.first_row + lax.broadcasted_iota(jnp.int32, (Q_ROWS, 1), 0)
            place = self.base + at + lax.broadcasted_iota(jnp.int32, shape, 1)
            live = (place <= row) & (place >= doc_start(row, self.ends))

        def score(head):
            rows = slice(head * Q_ROWS, (head + 1) * Q_ROWS)
            return jnp.dot(self.qs[rows], keys, preferred_element_type=jnp.float32)

        scores = score(0)
        for head in range(QPK):
            rows = slice(head * Q_ROWS, (head + 1) * Q_ROWS)
            upcoming = score(head + 1) if head + 1 < QPK else None
            if masked:
                scores = jnp.where(live, scores, MASKED)
            old_top = self.top[rows]
            new_top = jnp.maximum(old_top, jnp.max(scores, axis=1, keepdims=True))
            weights = jnp.exp2(scores - jnp.concatenate([new_top] * (size // HD), axis=1))
            part = jnp.dot(weights.astype(jnp.bfloat16), values, preferred_element_type=jnp.float32)
            factor = jnp.exp2(old_top - new_top)
            self.total[rows] = self.total[rows] * jnp.concatenate([factor, factor], axis=1) + part
            self.top[rows] = new_top
            scores = upcoming

    def cover(self, high, long):
        low = jnp.clip(self.first_start, 0, self.window) // K_SHORT * K_SHORT
        plain = (jnp.clip(self.last_start, 0, self.window) + K_SHORT - 1) // K_SHORT * K_SHORT
        for size, masked, until in ((long, False, plain), (long, True, low), (K_SHORT, True, low)):
            count = jnp.maximum(high - until, 0) // size
            lax.fori_loop(
                0,
                count,
                lambda step, _, high=high, size=size, masked=masked: self.run(high - (step + 1) * size, size, masked),
                None,
            )
            high = high - count * size

    def deliver(self, step, owner, stage, out, sems):
        piece = stage.shape[1]
        slots = Q_ROWS // piece
        for head in range(QPK):
            rows = slice(head * Q_ROWS, (head + 1) * Q_ROWS)
            done = (self.total[rows, :HD] / self.total[rows, HD:]).astype(jnp.bfloat16)
            for part in range(slots):
                stage[step * slots + part, :, head * HD : (head + 1) * HD] = done[part * piece : (part + 1) * piece]
        lax.fori_loop(0, slots, lambda part, _: sent(step * slots + part, owner, stage, out, sems).start(), None)


def sent(slot, owner, stage, out, sems):
    return pltpu.make_async_copy(stage.at[slot], out.at[owner[slot // out.shape[0], slot % out.shape[0]], slot // out.shape[0]], sems.at[slot])


def arrange(refs, turned, values):
    tokens = refs[0].shape[0]
    for index, ref in enumerate(refs):
        values[index * tokens : (index + 1) * tokens] = ref[:, :HD]

        def turn(tile, carry, ref=ref, index=index):
            rows = pl.ds(pl.multiple_of(tile * HD, HD), HD)
            turned[:, pl.ds(pl.multiple_of(index * tokens + tile * HD, HD), HD)] = ref[rows, HD:].T
            return carry

        lax.fori_loop(0, tokens // HD, turn, 0)


def keep(step, slot, top, total, tops, totals, kept, back):
    pairs = ((top.at[slot], tops.at[step]), (total.at[slot], totals.at[step]))
    if back:
        pairs = [pair[::-1] for pair in pairs]
    return [pltpu.make_async_copy(*pair, kept.at[slot, index]) for index, pair in enumerate(pairs)]


def far_blocks(place, ends, tokens):
    count = 0
    for step in range(tokens // Q_ROWS):
        count += (doc_start(place + step * Q_ROWS, ends) < place - tokens).astype(jnp.int32)
    return count


def ends_of(lengths):
    ends = [lengths[0]]
    for doc in range(1, lengths.shape[0]):
        ends.append(ends[-1] + lengths[doc])
    return ends


def near_kernel(at, lengths, owner, q_ref, own, near, out, tops, totals, turned, values, qs, top, total, stage, sems, kept):
    tokens = own.shape[0]
    step = pl.program_id(0)
    slot = lax.rem(step, 2)
    place = at[0]
    ends = ends_of(lengths)
    needed = far_blocks(place, ends, tokens)
    slots = Q_ROWS // stage.shape[1]

    @pl.when(step == 0)
    def _():
        arrange((near, own), turned, values)

    @pl.when((step >= 2) & (step - 2 < needed))
    def _():
        for copy in keep(step - 2, slot, top, total, tops, totals, kept, False):
            copy.wait()

    first_row = place + step * Q_ROWS
    block = Block(ends, first_row, place - tokens, 2 * tokens, turned, values, qs, top.at[slot], total.at[slot])
    block.load(q_ref)
    top[slot] = jnp.full(top.shape[1:], MASKED, jnp.float32)
    total[slot] = jnp.zeros(total.shape[1:], jnp.float32)
    long = min(K_LONG, tokens)
    high = tokens + (step + 1) * Q_ROWS - long
    block.run(high, long, True)
    block.cover(high, long)

    @pl.when(step >= needed)
    def _():
        block.deliver(step, owner, stage, out, sems)

    @pl.when(step < needed)
    def _():
        for copy in keep(step, slot, top, total, tops, totals, kept, False):
            copy.start()

    blocks = tokens // Q_ROWS

    @pl.when(step == blocks - 1)
    def _():
        for last in range(max(blocks - 2, 0), blocks):

            @pl.when(last < needed)
            def _(last=last):
                for copy in keep(last, last % 2, top, total, tops, totals, kept, False):
                    copy.wait()

        finish(needed * slots, blocks * slots, owner, stage, out, sems)


def finish(first, last, owner, stage, out, sems):
    lax.fori_loop(first, last, lambda slot, _: sent(slot, owner, stage, out, sems).wait(), None)


def far_kernel(at, lengths, owner, q_rows, tops, totals, begun, *refs):
    far, (out, held, fetched, turned, values, qs, top, total, stage, sems, kept, brought) = refs[:-12], refs[-12:]
    del begun
    tokens = q_rows.shape[0]
    window = tokens * len(far)
    place = at[0]
    ends = ends_of(lengths)
    needed = far_blocks(place, ends, tokens)

    def coming(step, slot):
        copies = keep(step, slot, top, total, tops, totals, kept, True)
        rows = pl.ds(pl.multiple_of(step * Q_ROWS, Q_ROWS), Q_ROWS)
        return copies + [pltpu.make_async_copy(q_rows.at[rows], held.at[slot], kept.at[slot, 2])]

    @pl.when(needed > 0)
    def _():
        whole = [pltpu.make_async_copy(ref, fetched.at[index], brought.at[index]) for index, ref in enumerate(far[::-1])]
        for copy in whole + coming(0, 0):
            copy.start()
        for copy in whole:
            copy.wait()
        arrange([fetched.at[index] for index in range(len(far))], turned, values)

    def one(step, carry):
        slot = lax.rem(step, 2)

        @pl.when(step + 1 < needed)
        def _():
            for copy in coming(step + 1, 1 - slot):
                copy.start()

        first_row = place + step * Q_ROWS
        block = Block(ends, first_row, place - tokens - window, window, turned, values, qs, top.at[slot], total.at[slot])
        for copy in coming(step, slot):
            copy.wait()
        block.load(held.at[slot])
        block.cover(window, min(K_LONG, tokens))
        block.deliver(step, owner, stage, out, sems)
        return carry

    lax.fori_loop(0, needed, one, 0)
    finish(0, needed * (Q_ROWS // stage.shape[1]), owner, stage, out, sems)


def attend(at, lengths, owner, n_owner, piece, query_rows, own, steps_back):
    tokens, features = query_rows.shape
    blocks = tokens // Q_ROWS
    near, far = steps_back[0], steps_back[1:]
    rows = QPK * Q_ROWS
    any_spec = pl.BlockSpec(memory_space=pl.ANY)
    paired_spec = pl.BlockSpec(own.shape, lambda i, *_: (0, 0))
    out_shape = jax.ShapeDtypeStruct((n_owner, tokens // (n_owner * piece), piece, features), jnp.bfloat16)
    state_shapes = [
        jax.ShapeDtypeStruct((blocks, rows, HD), jnp.float32),
        jax.ShapeDtypeStruct((blocks, rows, 2 * HD), jnp.float32),
    ]

    def scratch(window):
        return [
            pltpu.VMEM((HD, window), jnp.bfloat16),
            pltpu.VMEM((window, HD), jnp.bfloat16),
            pltpu.VMEM((rows, 2 * HD), jnp.bfloat16),
            pltpu.VMEM((2, rows, HD), jnp.float32),
            pltpu.VMEM((2, rows, 2 * HD), jnp.float32),
            pltpu.VMEM((tokens // piece, piece, features), jnp.bfloat16),
            pltpu.SemaphoreType.DMA((tokens // piece,)),
            pltpu.SemaphoreType.DMA((2, 3)),
        ]

    begun, tops, totals = pl.pallas_call(
        near_kernel,
        grid_spec=pltpu.PrefetchScalarGridSpec(
            num_scalar_prefetch=3,
            grid=(blocks,),
            in_specs=[pl.BlockSpec((Q_ROWS, features), lambda i, *_: (i, 0)), paired_spec, paired_spec],
            out_specs=[any_spec] * 3,
            scratch_shapes=scratch(2 * tokens),
        ),
        out_shape=[out_shape, *state_shapes],
        compiler_params=pltpu.CompilerParams(vmem_limit_bytes=VMEM),
        cost_estimate=pl.CostEstimate(flops=20_000_000_000, bytes_accessed=1 << 23, transcendentals=0),
        name="attend_near",
    )(at, lengths, owner, query_rows, own, near)
    if not far:
        return begun
    return pl.pallas_call(
        far_kernel,
        grid_spec=pltpu.PrefetchScalarGridSpec(
            num_scalar_prefetch=3,
            grid=(),
            in_specs=[any_spec] * (4 + len(far)),
            out_specs=any_spec,
            scratch_shapes=[
                pltpu.VMEM((2, Q_ROWS, features), jnp.bfloat16),
                pltpu.VMEM((len(far),) + own.shape, jnp.bfloat16),
                *scratch(tokens * len(far)),
                pltpu.SemaphoreType.DMA((len(far),)),
            ],
        ),
        out_shape=out_shape,
        input_output_aliases={6: 0},
        compiler_params=pltpu.CompilerParams(vmem_limit_bytes=VMEM),
        cost_estimate=pl.CostEstimate(flops=5_000_000_000, bytes_accessed=1 << 23, transcendentals=0),
        name="attend_far",
    )(at, lengths, owner, query_rows, tops, totals, begun, *far)


def moved_blocks(arrays, out_shape, routes, name):
    def kernel(*refs):
        ins, out, sems = refs[: len(arrays)], refs[-2], refs[-1]
        copies = [
            pltpu.make_async_copy(ins[index].at[here], out.at[there], sems.at[number])
            for number, (index, here, there) in enumerate(routes)
        ]
        for copy in copies:
            copy.start()
        for copy in copies:
            copy.wait()

    any_spec = pl.BlockSpec(memory_space=pl.ANY)
    return pl.pallas_call(
        kernel,
        in_specs=[any_spec] * len(arrays),
        out_specs=any_spec,
        out_shape=jax.ShapeDtypeStruct(out_shape, arrays[0].dtype),
        scratch_shapes=[pltpu.SemaphoreType.DMA((len(routes),))],
        name=name,
    )(*arrays)


def dealt(arrays, n_head, group, name):
    heads = n_head * group
    tok = arrays[0].shape[0]
    widths = [array.shape[1] // heads for array in arrays]
    routes = []
    for index, width in enumerate(widths):
        left = sum(widths[:index])
        for local in range(group):
            for head in range(n_head):
                source = (head * group + local) * width
                there = (local * n_head + head, slice(None), slice(left, left + width))
                routes.append((index, (slice(None), slice(source, source + width)), there))
    return moved_blocks(arrays, (heads, tok, sum(widths)), routes, name)


def laid_out(received, planes, group):
    _, rows, features = received.shape
    if group == 1:
        return received.reshape(planes * rows, features)
    routes = [
        (
            0,
            (plane * group + local,),
            (slice(plane * rows, (plane + 1) * rows), slice(local * features, (local + 1) * features)),
        )
        for plane in range(planes)
        for local in range(group)
    ]
    return moved_blocks([received], (planes * rows, group * features), routes, "lay_out")


def solution(mesh):
    n_ctx, n_head = mesh.shape["ctx"], mesh.shape["head"]

    def run(queries, keys, values, doc_lengths, piece_owner):
        group = keys.shape[1] // (HD * n_head)
        planes = n_ctx // group
        grouped = Mesh(mesh.devices.reshape(planes, group, n_head), ("plane", "local", "head"))
        rows = P(("plane", "local", "head"), None)

        def exchanged(split):
            moved = lax.all_to_all(split, ("local", "head"), split_axis=0, concat_axis=0, tiled=True)
            return moved.reshape(-1, split.shape[-1])

        def per_device(queries, keys, values, doc_lengths, piece_owner):
            paired = dealt([values, keys], n_head, group, "deal_keys")
            own = exchanged(paired)
            tokens = own.shape[0]
            reach = (MOST - 1) // tokens + 1
            up = [(plane, plane + 1) for plane in range(planes - 1)]
            steps_back = []
            moving = own
            for _ in range(reach):
                moving = lax.ppermute(moving, "plane", up)
                steps_back.append(moving)
            owner = lax.all_gather(piece_owner, "local", axis=0, tiled=True)
            split = dealt([queries], n_head, group, "deal_queries")
            split, owner = lax.optimization_barrier((split, owner))
            query_rows = exchanged(split)
            at = (lax.axis_index("plane") * tokens).astype(jnp.int32)[None]
            piece = tokens // (group * n_ctx)
            ordered = attend(at, doc_lengths, owner, n_ctx, piece, query_rows, own, steps_back)
            ordered = ordered.reshape(n_ctx, group * piece, -1)
            received = lax.all_to_all(ordered, ("plane", "local"), split_axis=0, concat_axis=0, tiled=True)
            return laid_out(received, planes, group)

        return jax.shard_map(
            per_device,
            mesh=grouped,
            in_specs=(rows, rows, rows, P(), P(("plane", "local"), None)),
            out_specs=P(("plane", "local"), "head"),
            check_vma=False,
        )(queries, keys, values, doc_lengths, piece_owner)

    return run
```

```python
import math

import jax
import jax.numpy as jnp
from jax import lax
from jax.experimental import pallas as pl
from jax.experimental.pallas import tpu as pltpu
from jax.sharding import Mesh
from jax.sharding import PartitionSpec as P

HD = 128
QPK = 4
MOST = 4096
Q_ROWS = 256
K_LONG = 1024
K_SHORT = 256
MASKED = -1e30
SCALE = math.log2(math.e) / math.sqrt(HD)
VMEM = 32 * 1024 * 1024


def doc_start(place, ends):
    start = jnp.zeros_like(place)
    for end in ends:
        start = jnp.maximum(start, jnp.where(end <= place, end, 0))
    return start


class Block:
    def __init__(self, ends, first_row, base, window, turned, values, qs, top, total):
        self.ends = ends
        self.first_row, self.base, self.window = first_row, base, window
        self.turned, self.values, self.qs, self.top, self.total = turned, values, qs, top, total
        self.first_start = doc_start(first_row, self.ends) - base
        self.last_start = doc_start(first_row + Q_ROWS - 1, self.ends) - base

    def load(self, q_ref):
        for head in range(QPK):
            scaled = q_ref[:, head * HD : (head + 1) * HD].astype(jnp.float32) * SCALE
            high = scaled.astype(jnp.bfloat16)
            rows = slice(head * Q_ROWS, (head + 1) * Q_ROWS)
            self.qs[rows, :HD] = high
            self.qs[rows, HD:] = (scaled - high.astype(jnp.float32)).astype(jnp.bfloat16)

    def run(self, at, size, masked):
        at = pl.multiple_of(at, K_SHORT)
        keys = self.turned[:, pl.ds(at, size)]
        keys = jnp.concatenate([keys, keys], axis=0)
        values = self.values[pl.ds(at, size), :]
        values = jnp.concatenate([values, jnp.ones_like(values)], axis=1)
        if masked:
            shape = (Q_ROWS, size)
            row = self.first_row + lax.broadcasted_iota(jnp.int32, (Q_ROWS, 1), 0)
            place = self.base + at + lax.broadcasted_iota(jnp.int32, shape, 1)
            live = (place <= row) & (place >= doc_start(row, self.ends))

        def score(head):
            rows = slice(head * Q_ROWS, (head + 1) * Q_ROWS)
            return jnp.dot(self.qs[rows], keys, preferred_element_type=jnp.float32)

        scores = score(0)
        for head in range(QPK):
            rows = slice(head * Q_ROWS, (head + 1) * Q_ROWS)
            upcoming = score(head + 1) if head + 1 < QPK else None
            if masked:
                scores = jnp.where(live, scores, MASKED)
            old_top = self.top[rows]
            new_top = jnp.maximum(old_top, jnp.max(scores, axis=1, keepdims=True))
            weights = jnp.exp2(scores - jnp.concatenate([new_top] * (size // HD), axis=1))
            part = jnp.dot(weights.astype(jnp.bfloat16), values, preferred_element_type=jnp.float32)
            factor = jnp.exp2(old_top - new_top)
            self.total[rows] = self.total[rows] * jnp.concatenate([factor, factor], axis=1) + part
            self.top[rows] = new_top
            scores = upcoming

    def cover(self, high, long):
        low = jnp.clip(self.first_start, 0, self.window) // K_SHORT * K_SHORT
        plain = (jnp.clip(self.last_start, 0, self.window) + K_SHORT - 1) // K_SHORT * K_SHORT
        for size, masked, until in ((long, False, plain), (long, True, low), (K_SHORT, True, low)):
            count = jnp.maximum(high - until, 0) // size
            lax.fori_loop(
                0,
                count,
                lambda step, _, high=high, size=size, masked=masked: self.run(high - (step + 1) * size, size, masked),
                None,
            )
            high = high - count * size

    def deliver(self, step, owner, stage, out, sems):
        piece = stage.shape[1]
        slots = Q_ROWS // piece
        for head in range(QPK):
            rows = slice(head * Q_ROWS, (head + 1) * Q_ROWS)
            done = (self.total[rows, :HD] / self.total[rows, HD:]).astype(jnp.bfloat16)
            for part in range(slots):
                stage[step * slots + part, :, head * HD : (head + 1) * HD] = done[part * piece : (part + 1) * piece]
        lax.fori_loop(0, slots, lambda part, _: sent(step * slots + part, owner, stage, out, sems).start(), None)


def sent(slot, owner, stage, out, sems):
    return pltpu.make_async_copy(stage.at[slot], out.at[owner[slot // out.shape[0], slot % out.shape[0]], slot // out.shape[0]], sems.at[slot])


def arrange(refs, turned, values):
    tokens = refs[0].shape[0]
    for index, ref in enumerate(refs):
        values[index * tokens : (index + 1) * tokens] = ref[:, :HD]

        def turn(tile, carry, ref=ref, index=index):
            rows = pl.ds(pl.multiple_of(tile * HD, HD), HD)
            turned[:, pl.ds(pl.multiple_of(index * tokens + tile * HD, HD), HD)] = ref[rows, HD:].T
            return carry

        lax.fori_loop(0, tokens // HD, turn, 0)


def keep(step, slot, top, total, tops, totals, kept, back):
    pairs = ((top.at[slot], tops.at[step]), (total.at[slot], totals.at[step]))
    if back:
        pairs = [pair[::-1] for pair in pairs]
    return [pltpu.make_async_copy(*pair, kept.at[slot, index]) for index, pair in enumerate(pairs)]


def far_blocks(place, ends, tokens):
    count = 0
    for step in range(tokens // Q_ROWS):
        count += (doc_start(place + step * Q_ROWS, ends) < place - tokens).astype(jnp.int32)
    return count


def ends_of(lengths):
    ends = [lengths[0]]
    for doc in range(1, lengths.shape[0]):
        ends.append(ends[-1] + lengths[doc])
    return ends


def near_kernel(at, lengths, owner, q_ref, own, near, out, tops, totals, turned, values, qs, top, total, stage, sems, kept):
    tokens = own.shape[0]
    step = pl.program_id(0)
    slot = lax.rem(step, 2)
    place = at[0]
    ends = ends_of(lengths)
    needed = far_blocks(place, ends, tokens)
    slots = Q_ROWS // stage.shape[1]

    @pl.when(step == 0)
    def _():
        arrange((near, own), turned, values)

    @pl.when((step >= 2) & (step - 2 < needed))
    def _():
        for copy in keep(step - 2, slot, top, total, tops, totals, kept, False):
            copy.wait()

    first_row = place + step * Q_ROWS
    block = Block(ends, first_row, place - tokens, 2 * tokens, turned, values, qs, top.at[slot], total.at[slot])
    block.load(q_ref)
    top[slot] = jnp.full(top.shape[1:], MASKED, jnp.float32)
    total[slot] = jnp.zeros(total.shape[1:], jnp.float32)
    long = min(K_LONG, tokens)
    high = tokens + (step + 1) * Q_ROWS - long
    block.run(high, long, True)
    block.cover(high, long)

    @pl.when(step >= needed)
    def _():
        block.deliver(step, owner, stage, out, sems)

    @pl.when(step < needed)
    def _():
        for copy in keep(step, slot, top, total, tops, totals, kept, False):
            copy.start()

    blocks = tokens // Q_ROWS

    @pl.when(step == blocks - 1)
    def _():
        for last in range(max(blocks - 2, 0), blocks):

            @pl.when(last < needed)
            def _(last=last):
                for copy in keep(last, last % 2, top, total, tops, totals, kept, False):
                    copy.wait()

        finish(needed * slots, blocks * slots, owner, stage, out, sems)


def finish(first, last, owner, stage, out, sems):
    lax.fori_loop(first, last, lambda slot, _: sent(slot, owner, stage, out, sems).wait(), None)


def far_kernel(at, lengths, owner, q_rows, tops, totals, begun, *refs):
    far, (out, held, fetched, turned, values, qs, top, total, stage, sems, kept, brought) = refs[:-12], refs[-12:]
    del begun
    tokens = q_rows.shape[0]
    window = tokens * len(far)
    place = at[0]
    ends = ends_of(lengths)
    needed = far_blocks(place, ends, tokens)

    def coming(step, slot):
        copies = keep(step, slot, top, total, tops, totals, kept, True)
        rows = pl.ds(pl.multiple_of(step * Q_ROWS, Q_ROWS), Q_ROWS)
        return copies + [pltpu.make_async_copy(q_rows.at[rows], held.at[slot], kept.at[slot, 2])]

    @pl.when(needed > 0)
    def _():
        whole = [pltpu.make_async_copy(ref, fetched.at[index], brought.at[index]) for index, ref in enumerate(far[::-1])]
        for copy in whole + coming(0, 0):
            copy.start()
        for copy in whole:
            copy.wait()
        arrange([fetched.at[index] for index in range(len(far))], turned, values)

    def one(step, carry):
        slot = lax.rem(step, 2)

        @pl.when(step + 1 < needed)
        def _():
            for copy in coming(step + 1, 1 - slot):
                copy.start()

        first_row = place + step * Q_ROWS
        block = Block(ends, first_row, place - tokens - window, window, turned, values, qs, top.at[slot], total.at[slot])
        for copy in coming(step, slot):
            copy.wait()
        block.load(held.at[slot])
        block.cover(window, min(K_LONG, tokens))
        block.deliver(step, owner, stage, out, sems)
        return carry

    lax.fori_loop(0, needed, one, 0)
    finish(0, needed * (Q_ROWS // stage.shape[1]), owner, stage, out, sems)


def attend(at, lengths, owner, n_owner, piece, query_rows, own, steps_back):
    tokens, features = query_rows.shape
    blocks = tokens // Q_ROWS
    near, far = steps_back[0], steps_back[1:]
    rows = QPK * Q_ROWS
    any_spec = pl.BlockSpec(memory_space=pl.ANY)
    paired_spec = pl.BlockSpec(own.shape, lambda i, *_: (0, 0))
    out_shape = jax.ShapeDtypeStruct((n_owner, tokens // (n_owner * piece), piece, features), jnp.bfloat16)
    state_shapes = [
        jax.ShapeDtypeStruct((blocks, rows, HD), jnp.float32),
        jax.ShapeDtypeStruct((blocks, rows, 2 * HD), jnp.float32),
    ]

    def scratch(window):
        return [
            pltpu.VMEM((HD, window), jnp.bfloat16),
            pltpu.VMEM((window, HD), jnp.bfloat16),
            pltpu.VMEM((rows, 2 * HD), jnp.bfloat16),
            pltpu.VMEM((2, rows, HD), jnp.float32),
            pltpu.VMEM((2, rows, 2 * HD), jnp.float32),
            pltpu.VMEM((tokens // piece, piece, features), jnp.bfloat16),
            pltpu.SemaphoreType.DMA((tokens // piece,)),
            pltpu.SemaphoreType.DMA((2, 3)),
        ]

    begun, tops, totals = pl.pallas_call(
        near_kernel,
        grid_spec=pltpu.PrefetchScalarGridSpec(
            num_scalar_prefetch=3,
            grid=(blocks,),
            in_specs=[pl.BlockSpec((Q_ROWS, features), lambda i, *_: (i, 0)), paired_spec, paired_spec],
            out_specs=[any_spec] * 3,
            scratch_shapes=scratch(2 * tokens),
        ),
        out_shape=[out_shape, *state_shapes],
        compiler_params=pltpu.CompilerParams(vmem_limit_bytes=VMEM),
        cost_estimate=pl.CostEstimate(flops=20_000_000_000, bytes_accessed=1 << 23, transcendentals=0),
        name="attend_near",
    )(at, lengths, owner, query_rows, own, near)
    if not far:
        return begun
    return pl.pallas_call(
        far_kernel,
        grid_spec=pltpu.PrefetchScalarGridSpec(
            num_scalar_prefetch=3,
            grid=(),
            in_specs=[any_spec] * (4 + len(far)),
            out_specs=any_spec,
            scratch_shapes=[
                pltpu.VMEM((2, Q_ROWS, features), jnp.bfloat16),
                pltpu.VMEM((len(far),) + own.shape, jnp.bfloat16),
                *scratch(tokens * len(far)),
                pltpu.SemaphoreType.DMA((len(far),)),
            ],
        ),
        out_shape=out_shape,
        input_output_aliases={6: 0},
        compiler_params=pltpu.CompilerParams(vmem_limit_bytes=VMEM),
        cost_estimate=pl.CostEstimate(flops=5_000_000_000, bytes_accessed=1 << 23, transcendentals=0),
        name="attend_far",
    )(at, lengths, owner, query_rows, tops, totals, begun, *far)


def dealt(arrays, n_head, group, name):
    heads = n_head * group
    tok = arrays[0].shape[0]
    widths = [array.shape[1] // heads for array in arrays]
    step_rows = max(tok // 4, 16)

    def kernel(*refs):
        out = refs[-1]
        for index, width in enumerate(widths):
            left = sum(widths[:index])
            for head in range(n_head):
                for local in range(group):
                    source = (head * group + local) * width
                    out[local * n_head + head, :, left : left + width] = refs[index][:, source : source + width]

    return pl.pallas_call(
        kernel,
        grid=(tok // step_rows,),
        in_specs=[pl.BlockSpec((step_rows, array.shape[1]), lambda i: (i, 0)) for array in arrays],
        out_specs=pl.BlockSpec((heads, step_rows, sum(widths)), lambda i: (0, i, 0)),
        out_shape=jax.ShapeDtypeStruct((heads, tok, sum(widths)), arrays[0].dtype),
        compiler_params=pltpu.CompilerParams(vmem_limit_bytes=VMEM),
        name=name,
    )(*arrays)


def laid_out(received, planes, group):
    _, rows, features = received.shape
    if group == 1:
        return received.reshape(planes * rows, features)

    def kernel(blocks, out):
        for local in range(group):
            out[:, local * features : (local + 1) * features] = blocks[local]

    return pl.pallas_call(
        kernel,
        grid=(planes,),
        in_specs=[pl.BlockSpec((group, rows, features), lambda i: (i, 0, 0))],
        out_specs=pl.BlockSpec((rows, group * features), lambda i: (i, 0)),
        out_shape=jax.ShapeDtypeStruct((planes * rows, group * features), received.dtype),
        compiler_params=pltpu.CompilerParams(vmem_limit_bytes=VMEM),
        name="lay_out",
    )(received)


def solution(mesh):
    n_ctx, n_head = mesh.shape["ctx"], mesh.shape["head"]

    def run(queries, keys, values, doc_lengths, piece_owner):
        group = keys.shape[1] // (HD * n_head)
        planes = n_ctx // group
        grouped = Mesh(mesh.devices.reshape(planes, group, n_head), ("plane", "local", "head"))
        rows = P(("plane", "local", "head"), None)

        def exchanged(split):
            moved = lax.all_to_all(split, ("local", "head"), split_axis=0, concat_axis=0, tiled=True)
            return moved.reshape(-1, split.shape[-1])

        def per_device(queries, keys, values, doc_lengths, piece_owner):
            paired = dealt([values, keys], n_head, group, "deal_keys")
            own = exchanged(paired)
            tokens = own.shape[0]
            reach = (MOST - 1) // tokens + 1
            up = [(plane, plane + 1) for plane in range(planes - 1)]
            steps_back = []
            moving = own
            for _ in range(reach):
                moving = lax.ppermute(moving, "plane", up)
                steps_back.append(moving)
            owner = lax.all_gather(piece_owner, "local", axis=0, tiled=True)
            split = dealt([queries], n_head, group, "deal_queries")
            split, owner = lax.optimization_barrier((split, owner))
            query_rows = exchanged(split)
            at = (lax.axis_index("plane") * tokens).astype(jnp.int32)[None]
            piece = tokens // (group * n_ctx)
            ordered = attend(at, doc_lengths, owner, n_ctx, piece, query_rows, own, steps_back)
            ordered = ordered.reshape(n_ctx, group * piece, -1)
            received = lax.all_to_all(ordered, ("plane", "local"), split_axis=0, concat_axis=0, tiled=True)
            return laid_out(received, planes, group)

        return jax.shard_map(
            per_device,
            mesh=grouped,
            in_specs=(rows, rows, rows, P(), P(("plane", "local"), None)),
            out_specs=P(("plane", "local"), "head"),
            check_vma=False,
        )(queries, keys, values, doc_lengths, piece_owner)

    return run
```

```python
import math

import jax
import jax.numpy as jnp
from jax import lax
from jax.experimental import pallas as pl
from jax.experimental.pallas import tpu as pltpu
from jax.sharding import Mesh
from jax.sharding import PartitionSpec as P

HD = 128
QPK = 4
MOST = 4096
Q_ROWS = 256
K_LONG = 1024
K_SHORT = 256
MASKED = -1e30
SCALE = math.log2(math.e) / math.sqrt(HD)
VMEM = 32 * 1024 * 1024
VMEM_FIRST = 60 * 1024 * 1024


def doc_start(place, ends):
    start = jnp.zeros_like(place)
    for end in ends:
        start = jnp.maximum(start, jnp.where(end <= place, end, 0))
    return start


class Block:
    def __init__(self, ends, first_row, base, pairs, qs, top, total):
        self.ends = ends
        self.first_row, self.base, self.window = first_row, base, pairs.shape[0]
        self.pairs, self.qs, self.top, self.total = pairs, qs, top, total
        self.first_start = doc_start(first_row, self.ends) - base
        self.last_start = doc_start(first_row + Q_ROWS - 1, self.ends) - base

    def load(self, q_ref):
        for head in range(QPK):
            scaled = q_ref[:, head * HD : (head + 1) * HD].astype(jnp.float32) * SCALE
            high = scaled.astype(jnp.bfloat16)
            rows = slice(head * Q_ROWS, (head + 1) * Q_ROWS)
            self.qs[rows, :HD] = high
            self.qs[rows, HD:] = (scaled - high.astype(jnp.float32)).astype(jnp.bfloat16)

    def run(self, at, size, masked):
        at = pl.multiple_of(at, K_SHORT)
        values = self.pairs[pl.ds(at, size), :HD]
        keys = self.pairs[pl.ds(at, size), HD:]
        keys = jnp.concatenate([keys, keys], axis=1)
        values = jnp.concatenate([values, jnp.ones_like(values)], axis=1)
        if masked:
            shape = (Q_ROWS, size)
            row = self.first_row + lax.broadcasted_iota(jnp.int32, (Q_ROWS, 1), 0)
            place = self.base + at + lax.broadcasted_iota(jnp.int32, shape, 1)
            live = (place <= row) & (place >= doc_start(row, self.ends))

        def score(head):
            rows = slice(head * Q_ROWS, (head + 1) * Q_ROWS)
            return lax.dot_general(
                self.qs[rows], keys, (((1,), (1,)), ((), ())), preferred_element_type=jnp.float32
            )

        scores = score(0)
        for head in range(QPK):
            rows = slice(head * Q_ROWS, (head + 1) * Q_ROWS)
            upcoming = score(head + 1) if head + 1 < QPK else None
            if masked:
                scores = jnp.where(live, scores, MASKED)
            old_top = self.top[rows]
            new_top = jnp.maximum(old_top, jnp.max(scores, axis=1, keepdims=True))
            weights = jnp.exp2(scores - jnp.concatenate([new_top] * (size // HD), axis=1))
            part = jnp.dot(weights.astype(jnp.bfloat16), values, preferred_element_type=jnp.float32)
            factor = jnp.exp2(old_top - new_top)
            self.total[rows] = self.total[rows] * jnp.concatenate([factor, factor], axis=1) + part
            self.top[rows] = new_top
            scores = upcoming

    def cover(self, high, long):
        low = jnp.clip(self.first_start, 0, self.window) // K_SHORT * K_SHORT
        plain = (jnp.clip(self.last_start, 0, self.window) + K_SHORT - 1) // K_SHORT * K_SHORT
        middle = max(long // 2, K_SHORT)
        for size, masked, until in ((long, False, plain), (long, True, low), (middle, True, low), (K_SHORT, True, low)):
            count = jnp.maximum(high - until, 0) // size
            lax.fori_loop(
                0,
                count,
                lambda step, _, high=high, size=size, masked=masked: self.run(high - (step + 1) * size, size, masked),
                None,
            )
            high = high - count * size

    def deliver(self, step, owner, stage, out, sems):
        piece = stage.shape[1]
        slots = Q_ROWS // piece
        for head in range(QPK):
            rows = slice(head * Q_ROWS, (head + 1) * Q_ROWS)
            done = (self.total[rows, :HD] / self.total[rows, HD:]).astype(jnp.bfloat16)
            for part in range(slots):
                stage[step * slots + part, :, head * HD : (head + 1) * HD] = done[part * piece : (part + 1) * piece]
        lax.fori_loop(0, slots, lambda part, _: sent(step * slots + part, owner, stage, out, sems).start(), None)


def sent(slot, owner, stage, out, sems):
    return pltpu.make_async_copy(stage.at[slot], out.at[owner[slot // out.shape[0], slot % out.shape[0]], slot // out.shape[0]], sems.at[slot])


def keep(step, slot, top, total, tops, totals, kept, back):
    pairs = ((top.at[slot], tops.at[step]), (total.at[slot], totals.at[step]))
    if back:
        pairs = [pair[::-1] for pair in pairs]
    return [pltpu.make_async_copy(*pair, kept.at[slot, index]) for index, pair in enumerate(pairs)]


def far_blocks(place, ends, tokens):
    count = 0
    for step in range(tokens // Q_ROWS):
        count += (doc_start(place + step * Q_ROWS, ends) < place - tokens).astype(jnp.int32)
    return count


def ends_of(lengths):
    ends = [lengths[0]]
    for doc in range(1, lengths.shape[0]):
        ends.append(ends[-1] + lengths[doc])
    return ends


def near_kernel(at, lengths, owner, q_ref, own, near, out, tops, totals, pairs, qs, top, total, stage, sems, kept, brought):
    tokens = own.shape[0]
    step = pl.program_id(0)
    slot = lax.rem(step, 2)
    place = at[0]
    ends = ends_of(lengths)
    needed = far_blocks(place, ends, tokens)
    slots = Q_ROWS // stage.shape[1]

    @pl.when(step == 0)
    def _():
        copies = [
            pltpu.make_async_copy(ref, pairs.at[index * tokens : (index + 1) * tokens], brought.at[index])
            for index, ref in enumerate((near, own))
        ]
        for copy in copies:
            copy.start()
        for copy in copies:
            copy.wait()

    @pl.when((step >= 2) & (step - 2 < needed))
    def _():
        for copy in keep(step - 2, slot, top, total, tops, totals, kept, False):
            copy.wait()

    first_row = place + step * Q_ROWS
    block = Block(ends, first_row, place - tokens, pairs, qs, top.at[slot], total.at[slot])
    block.load(q_ref)
    top[slot] = jnp.full(top.shape[1:], MASKED, jnp.float32)
    total[slot] = jnp.zeros(total.shape[1:], jnp.float32)
    long = min(K_LONG, tokens)
    high = tokens + (step + 1) * Q_ROWS - long
    block.run(high, long, True)
    block.cover(high, long)

    @pl.when(step >= needed)
    def _():
        block.deliver(step, owner, stage, out, sems)

    @pl.when(step < needed)
    def _():
        for copy in keep(step, slot, top, total, tops, totals, kept, False):
            copy.start()

    blocks = tokens // Q_ROWS

    @pl.when(step == blocks - 1)
    def _():
        for last in range(max(blocks - 2, 0), blocks):

            @pl.when(last < needed)
            def _(last=last):
                for copy in keep(last, last % 2, top, total, tops, totals, kept, False):
                    copy.wait()

        finish(needed * slots, blocks * slots, owner, stage, out, sems)


def finish(first, last, owner, stage, out, sems):
    lax.fori_loop(first, last, lambda slot, _: sent(slot, owner, stage, out, sems).wait(), None)


def far_kernel(at, lengths, owner, q_rows, tops, totals, begun, *refs):
    far, (out, held, pairs, qs, top, total, stage, sems, kept, brought) = refs[:-10], refs[-10:]
    del begun
    tokens = q_rows.shape[0]
    window = tokens * len(far)
    place = at[0]
    ends = ends_of(lengths)
    needed = far_blocks(place, ends, tokens)

    def coming(step, slot):
        copies = keep(step, slot, top, total, tops, totals, kept, True)
        rows = pl.ds(pl.multiple_of(step * Q_ROWS, Q_ROWS), Q_ROWS)
        return copies + [pltpu.make_async_copy(q_rows.at[rows], held.at[slot], kept.at[slot, 2])]

    @pl.when(needed > 0)
    def _():
        whole = [
            pltpu.make_async_copy(ref, pairs.at[index * tokens : (index + 1) * tokens], brought.at[index])
            for index, ref in enumerate(far[::-1])
        ]
        for copy in whole + coming(0, 0):
            copy.start()
        for copy in whole:
            copy.wait()

    def one(step, carry):
        slot = lax.rem(step, 2)

        @pl.when(step + 1 < needed)
        def _():
            for copy in coming(step + 1, 1 - slot):
                copy.start()

        first_row = place + step * Q_ROWS
        block = Block(ends, first_row, place - tokens - window, pairs, qs, top.at[slot], total.at[slot])
        for copy in coming(step, slot):
            copy.wait()
        block.load(held.at[slot])
        block.cover(window, min(K_LONG, tokens))
        block.deliver(step, owner, stage, out, sems)
        return carry

    lax.fori_loop(0, needed, one, 0)
    finish(0, needed * (Q_ROWS // stage.shape[1]), owner, stage, out, sems)


def attend(at, lengths, owner, n_owner, piece, query_rows, own, steps_back):
    tokens, features = query_rows.shape
    blocks = tokens // Q_ROWS
    near, far = steps_back[0], steps_back[1:]
    rows = QPK * Q_ROWS
    any_spec = pl.BlockSpec(memory_space=pl.ANY)
    out_shape = jax.ShapeDtypeStruct((n_owner, tokens // (n_owner * piece), piece, features), jnp.bfloat16)
    state_shapes = [
        jax.ShapeDtypeStruct((blocks, rows, HD), jnp.float32),
        jax.ShapeDtypeStruct((blocks, rows, 2 * HD), jnp.float32),
    ]

    def scratch(window):
        return [
            pltpu.VMEM((window, 2 * HD), jnp.bfloat16),
            pltpu.VMEM((rows, 2 * HD), jnp.bfloat16),
            pltpu.VMEM((2, rows, HD), jnp.float32),
            pltpu.VMEM((2, rows, 2 * HD), jnp.float32),
            pltpu.VMEM((tokens // piece, piece, features), jnp.bfloat16),
            pltpu.SemaphoreType.DMA((tokens // piece,)),
            pltpu.SemaphoreType.DMA((2, 3)),
            pltpu.SemaphoreType.DMA((window // tokens,)),
        ]

    begun, tops, totals = pl.pallas_call(
        near_kernel,
        grid_spec=pltpu.PrefetchScalarGridSpec(
            num_scalar_prefetch=3,
            grid=(blocks,),
            in_specs=[pl.BlockSpec((Q_ROWS, features), lambda i, *_: (i, 0)), any_spec, any_spec],
            out_specs=[any_spec] * 3,
            scratch_shapes=scratch(2 * tokens),
        ),
        out_shape=[out_shape, *state_shapes],
        compiler_params=pltpu.CompilerParams(vmem_limit_bytes=VMEM),
        cost_estimate=pl.CostEstimate(flops=20_000_000_000, bytes_accessed=1 << 23, transcendentals=0),
        name="attend_near",
    )(at, lengths, owner, query_rows, own, near)
    if not far:
        return begun
    return pl.pallas_call(
        far_kernel,
        grid_spec=pltpu.PrefetchScalarGridSpec(
            num_scalar_prefetch=3,
            grid=(),
            in_specs=[any_spec] * (4 + len(far)),
            out_specs=any_spec,
            scratch_shapes=[
                pltpu.VMEM((2, Q_ROWS, features), jnp.bfloat16),
                *scratch(tokens * len(far)),
            ],
        ),
        out_shape=out_shape,
        input_output_aliases={6: 0},
        compiler_params=pltpu.CompilerParams(vmem_limit_bytes=VMEM),
        cost_estimate=pl.CostEstimate(flops=5_000_000_000, bytes_accessed=1 << 23, transcendentals=0),
        name="attend_far",
    )(at, lengths, owner, query_rows, tops, totals, begun, *far)


def dealt(arrays, n_head, group, name):
    heads = n_head * group
    tok = arrays[0].shape[0]
    widths = [array.shape[1] // heads for array in arrays]
    step_rows = max(tok // 4, 16)

    def kernel(*refs):
        out = refs[-1]
        for index, width in enumerate(widths):
            left = sum(widths[:index])
            for head in range(n_head):
                for local in range(group):
                    source = (head * group + local) * width
                    out[local * n_head + head, :, left : left + width] = refs[index][:, source : source + width]

    return pl.pallas_call(
        kernel,
        grid=(tok // step_rows,),
        in_specs=[pl.BlockSpec((step_rows, array.shape[1]), lambda i: (i, 0)) for array in arrays],
        out_specs=pl.BlockSpec((heads, step_rows, sum(widths)), lambda i: (0, i, 0)),
        out_shape=jax.ShapeDtypeStruct((heads, tok, sum(widths)), arrays[0].dtype),
        compiler_params=pltpu.CompilerParams(vmem_limit_bytes=VMEM_FIRST),
        name=name,
    )(*arrays)


def laid_out(received, planes, group):
    _, rows, features = received.shape
    if group == 1:
        return received.reshape(planes * rows, features)

    def kernel(blocks, out):
        for local in range(group):
            out[:, local * features : (local + 1) * features] = blocks[local]

    return pl.pallas_call(
        kernel,
        grid=(planes,),
        in_specs=[pl.BlockSpec((group, rows, features), lambda i: (i, 0, 0))],
        out_specs=pl.BlockSpec((rows, group * features), lambda i: (i, 0)),
        out_shape=jax.ShapeDtypeStruct((planes * rows, group * features), received.dtype),
        compiler_params=pltpu.CompilerParams(vmem_limit_bytes=VMEM),
        name="lay_out",
    )(received)


def solution(mesh):
    n_ctx, n_head = mesh.shape["ctx"], mesh.shape["head"]

    def run(queries, keys, values, doc_lengths, piece_owner):
        group = keys.shape[1] // (HD * n_head)
        planes = n_ctx // group
        grouped = Mesh(mesh.devices.reshape(planes, group, n_head), ("plane", "local", "head"))
        rows = P(("plane", "local", "head"), None)

        def exchanged(split):
            moved = lax.all_to_all(split, ("local", "head"), split_axis=0, concat_axis=0, tiled=True)
            return moved.reshape(-1, split.shape[-1])

        def per_device(queries, keys, values, doc_lengths, piece_owner):
            paired = dealt([values, keys], n_head, group, "deal_keys")
            own = exchanged(paired)
            tokens = own.shape[0]
            reach = (MOST - 1) // tokens + 1
            up = [(plane, plane + 1) for plane in range(planes - 1)]
            steps_back = []
            moving = own
            for _ in range(reach):
                moving = lax.ppermute(moving, "plane", up)
                steps_back.append(moving)
            owner = lax.all_gather(piece_owner, "local", axis=0, tiled=True)
            split = dealt([queries], n_head, group, "deal_queries")
            split, owner = lax.optimization_barrier((split, owner))
            query_rows = exchanged(split)
            at = (lax.axis_index("plane") * tokens).astype(jnp.int32)[None]
            piece = tokens // (group * n_ctx)
            ordered = attend(at, doc_lengths, owner, n_ctx, piece, query_rows, own, steps_back)
            ordered = ordered.reshape(n_ctx, group * piece, -1)
            received = lax.all_to_all(ordered, ("plane", "local"), split_axis=0, concat_axis=0, tiled=True)
            return laid_out(received, planes, group)

        return jax.shard_map(
            per_device,
            mesh=grouped,
            in_specs=(rows, rows, rows, P(), P(("plane", "local"), None)),
            out_specs=P(("plane", "local"), "head"),
            check_vma=False,
        )(queries, keys, values, doc_lengths, piece_owner)

    return run
```

```python
import math

import jax
import jax.numpy as jnp
from jax import lax
from jax.experimental import pallas as pl
from jax.experimental.pallas import tpu as pltpu
from jax.sharding import Mesh
from jax.sharding import PartitionSpec as P

HD = 128
MOST = 4096
PARTS = 2
Q_ROWS = 512
CHUNK = 256
K_LONG = 1024
K_SHORT = 256
MASKED = -1e30
SCALE = math.log2(math.e) / math.sqrt(HD)
VMEM = 32 * 1024 * 1024
STEPS = 4
VMEM_FIRST = 60 * 1024 * 1024


def doc_start(place, ends):
    start = jnp.zeros_like(place)
    for end in ends:
        start = jnp.maximum(start, jnp.where(end <= place, end, 0))
    return start


class Block:
    def __init__(self, ends, first_row, base, pairs, qs, top, total):
        self.ends = ends
        self.first_row, self.base, self.window = first_row, base, pairs.shape[0]
        self.pairs, self.qs, self.top, self.total = pairs, qs, top, total
        self.heads = qs.shape[0] // Q_ROWS
        self.first_start = doc_start(first_row, self.ends) - base
        self.last_start = doc_start(first_row + Q_ROWS - 1, self.ends) - base

    def load(self, q_ref):
        for head in range(self.heads):
            scaled = q_ref[:, head * HD : (head + 1) * HD].astype(jnp.float32) * SCALE
            high = scaled.astype(jnp.bfloat16)
            rows = slice(head * Q_ROWS, (head + 1) * Q_ROWS)
            self.qs[rows, :HD] = high
            self.qs[rows, HD:] = (scaled - high.astype(jnp.float32)).astype(jnp.bfloat16)

    def run(self, at, size, masked):
        at = pl.multiple_of(at, K_SHORT)
        values = self.pairs[pl.ds(at, size), :HD]
        keys = self.pairs[pl.ds(at, size), HD:]
        keys = jnp.concatenate([keys, keys], axis=1)
        values = jnp.concatenate([values, jnp.ones_like(values)], axis=1)
        lives = []
        if masked:
            place = self.base + at + lax.broadcasted_iota(jnp.int32, (CHUNK, size), 1)
            for first in range(0, Q_ROWS, CHUNK):
                row = self.first_row + first + lax.broadcasted_iota(jnp.int32, (CHUNK, 1), 0)
                lives.append((place <= row) & (place >= doc_start(row, self.ends)))

        def score(chunk):
            return lax.dot_general(
                self.qs[chunk * CHUNK : (chunk + 1) * CHUNK],
                keys,
                (((1,), (1,)), ((), ())),
                preferred_element_type=jnp.float32,
            )

        chunks = self.heads * Q_ROWS // CHUNK
        scores = score(0)
        for chunk in range(chunks):
            rows = slice(chunk * CHUNK, (chunk + 1) * CHUNK)
            upcoming = score(chunk + 1) if chunk + 1 < chunks else None
            if masked:
                scores = jnp.where(lives[chunk % (Q_ROWS // CHUNK)], scores, MASKED)
            old_top = self.top[rows]
            new_top = jnp.maximum(old_top, jnp.max(scores, axis=1, keepdims=True))
            weights = jnp.exp2(scores - jnp.concatenate([new_top] * (size // HD), axis=1))
            part = jnp.dot(weights.astype(jnp.bfloat16), values, preferred_element_type=jnp.float32)
            factor = jnp.exp2(old_top - new_top)
            self.total[rows] = self.total[rows] * jnp.concatenate([factor, factor], axis=1) + part
            self.top[rows] = new_top
            scores = upcoming

    def cover(self, high, long):
        low = jnp.clip(self.first_start, 0, self.window) // K_SHORT * K_SHORT
        plain = (jnp.clip(self.last_start, 0, self.window) + K_SHORT - 1) // K_SHORT * K_SHORT
        middle = max(long // 2, K_SHORT)
        for size, masked, until in ((long, False, plain), (long, True, low), (middle, True, low), (K_SHORT, True, low)):
            count = jnp.maximum(high - until, 0) // size
            lax.fori_loop(
                0,
                count,
                lambda step, _, high=high, size=size, masked=masked: self.run(high - (step + 1) * size, size, masked),
                None,
            )
            high = high - count * size

    def deliver(self, step, owner, stage, out, sems):
        piece = stage.shape[1]
        slots = Q_ROWS // piece
        for head in range(self.heads):
            rows = slice(head * Q_ROWS, (head + 1) * Q_ROWS)
            done = (self.total[rows, :HD] / self.total[rows, HD:]).astype(jnp.bfloat16)
            for part in range(slots):
                stage[step * slots + part, :, head * HD : (head + 1) * HD] = done[part * piece : (part + 1) * piece]
        lax.fori_loop(0, slots, lambda part, _: sent(step * slots + part, owner, stage, out, sems).start(), None)


def sent(slot, owner, stage, out, sems):
    return pltpu.make_async_copy(stage.at[slot], out.at[owner[slot // out.shape[0], slot % out.shape[0]], slot // out.shape[0]], sems.at[slot])


def keep(step, slot, top, total, tops, totals, kept, back):
    pairs = ((top.at[slot], tops.at[step]), (total.at[slot], totals.at[step]))
    if back:
        pairs = [pair[::-1] for pair in pairs]
    return [pltpu.make_async_copy(*pair, kept.at[slot, index]) for index, pair in enumerate(pairs)]


def far_blocks(place, ends, tokens):
    count = 0
    for step in range(tokens // Q_ROWS):
        count += (doc_start(place + step * Q_ROWS, ends) < place - tokens).astype(jnp.int32)
    return count


def ends_of(lengths):
    ends = [lengths[0]]
    for doc in range(1, lengths.shape[0]):
        ends.append(ends[-1] + lengths[doc])
    return ends


def near_kernel(at, lengths, owner, q_ref, own, near, out, tops, totals, pairs, qs, top, total, stage, sems, kept, brought):
    tokens = own.shape[0]
    step = pl.program_id(0)
    slot = lax.rem(step, 2)
    place = at[0]
    ends = ends_of(lengths)
    needed = far_blocks(place, ends, tokens)
    slots = Q_ROWS // stage.shape[1]

    @pl.when(step == 0)
    def _():
        copies = [
            pltpu.make_async_copy(ref, pairs.at[index * tokens : (index + 1) * tokens], brought.at[index])
            for index, ref in enumerate((near, own))
        ]
        for copy in copies:
            copy.start()
        for copy in copies:
            copy.wait()

    @pl.when((step >= 2) & (step - 2 < needed))
    def _():
        for copy in keep(step - 2, slot, top, total, tops, totals, kept, False):
            copy.wait()

    first_row = place + step * Q_ROWS
    block = Block(ends, first_row, place - tokens, pairs, qs, top.at[slot], total.at[slot])
    block.load(q_ref)
    top[slot] = jnp.full(top.shape[1:], MASKED, jnp.float32)
    total[slot] = jnp.zeros(total.shape[1:], jnp.float32)
    long = min(K_LONG, tokens)
    high = tokens + (step + 1) * Q_ROWS - long
    block.run(high, long, True)
    block.cover(high, long)

    @pl.when(step >= needed)
    def _():
        block.deliver(step, owner, stage, out, sems)

    @pl.when(step < needed)
    def _():
        for copy in keep(step, slot, top, total, tops, totals, kept, False):
            copy.start()

    blocks = tokens // Q_ROWS

    @pl.when(step == blocks - 1)
    def _():
        for last in range(max(blocks - 2, 0), blocks):

            @pl.when(last < needed)
            def _(last=last):
                for copy in keep(last, last % 2, top, total, tops, totals, kept, False):
                    copy.wait()

        finish(needed * slots, blocks * slots, owner, stage, out, sems)


def finish(first, last, owner, stage, out, sems):
    lax.fori_loop(first, last, lambda slot, _: sent(slot, owner, stage, out, sems).wait(), None)


def far_kernel(at, lengths, owner, q_rows, tops, totals, begun, *refs):
    far, (out, held, pairs, qs, top, total, stage, sems, kept, brought) = refs[:-10], refs[-10:]
    del begun
    tokens = q_rows.shape[0]
    window = tokens * len(far)
    place = at[0]
    ends = ends_of(lengths)
    needed = far_blocks(place, ends, tokens)

    def coming(step, slot):
        copies = keep(step, slot, top, total, tops, totals, kept, True)
        rows = pl.ds(pl.multiple_of(step * Q_ROWS, Q_ROWS), Q_ROWS)
        return copies + [pltpu.make_async_copy(q_rows.at[rows], held.at[slot], kept.at[slot, 2])]

    @pl.when(needed > 0)
    def _():
        whole = [
            pltpu.make_async_copy(ref, pairs.at[index * tokens : (index + 1) * tokens], brought.at[index])
            for index, ref in enumerate(far[::-1])
        ]
        for copy in whole + coming(0, 0):
            copy.start()
        for copy in whole:
            copy.wait()

    def one(step, carry):
        slot = lax.rem(step, 2)

        @pl.when(step + 1 < needed)
        def _():
            for copy in coming(step + 1, 1 - slot):
                copy.start()

        first_row = place + step * Q_ROWS
        block = Block(ends, first_row, place - tokens - window, pairs, qs, top.at[slot], total.at[slot])
        for copy in coming(step, slot):
            copy.wait()
        block.load(held.at[slot])
        block.cover(window, min(K_LONG, tokens))
        block.deliver(step, owner, stage, out, sems)
        return carry

    lax.fori_loop(0, needed, one, 0)
    finish(0, needed * (Q_ROWS // stage.shape[1]), owner, stage, out, sems)


def attend(at, lengths, owner, n_owner, piece, query_rows, own, steps_back):
    tokens, features = query_rows.shape
    blocks = tokens // Q_ROWS
    near, far = steps_back[0], steps_back[1:]
    rows = features // HD * Q_ROWS
    any_spec = pl.BlockSpec(memory_space=pl.ANY)
    out_shape = jax.ShapeDtypeStruct((n_owner, tokens // (n_owner * piece), piece, features), jnp.bfloat16)
    state_shapes = [
        jax.ShapeDtypeStruct((blocks, rows, HD), jnp.float32),
        jax.ShapeDtypeStruct((blocks, rows, 2 * HD), jnp.float32),
    ]

    def scratch(window):
        return [
            pltpu.VMEM((window, 2 * HD), jnp.bfloat16),
            pltpu.VMEM((rows, 2 * HD), jnp.bfloat16),
            pltpu.VMEM((2, rows, HD), jnp.float32),
            pltpu.VMEM((2, rows, 2 * HD), jnp.float32),
            pltpu.VMEM((tokens // piece, piece, features), jnp.bfloat16),
            pltpu.SemaphoreType.DMA((tokens // piece,)),
            pltpu.SemaphoreType.DMA((2, 3)),
            pltpu.SemaphoreType.DMA((window // tokens,)),
        ]

    begun, tops, totals = pl.pallas_call(
        near_kernel,
        grid_spec=pltpu.PrefetchScalarGridSpec(
            num_scalar_prefetch=3,
            grid=(blocks,),
            in_specs=[pl.BlockSpec((Q_ROWS, features), lambda i, *_: (i, 0)), any_spec, any_spec],
            out_specs=[any_spec] * 3,
            scratch_shapes=scratch(2 * tokens),
        ),
        out_shape=[out_shape, *state_shapes],
        compiler_params=pltpu.CompilerParams(vmem_limit_bytes=VMEM_FIRST),
        cost_estimate=pl.CostEstimate(flops=20_000_000_000, bytes_accessed=1 << 23, transcendentals=0),
        name="attend_near",
    )(at, lengths, owner, query_rows, own, near)
    if not far:
        return begun
    return pl.pallas_call(
        far_kernel,
        grid_spec=pltpu.PrefetchScalarGridSpec(
            num_scalar_prefetch=3,
            grid=(),
            in_specs=[any_spec] * (4 + len(far)),
            out_specs=any_spec,
            scratch_shapes=[
                pltpu.VMEM((2, Q_ROWS, features), jnp.bfloat16),
                *scratch(tokens * len(far)),
            ],
        ),
        out_shape=out_shape,
        input_output_aliases={6: 0},
        compiler_params=pltpu.CompilerParams(vmem_limit_bytes=VMEM_FIRST),
        cost_estimate=pl.CostEstimate(flops=5_000_000_000, bytes_accessed=1 << 23, transcendentals=0),
        name="attend_far",
    )(at, lengths, owner, query_rows, tops, totals, begun, *far)


def dealt(arrays, n_head, group, parts, name):
    heads = n_head * group
    tok = arrays[0].shape[0]
    widths = [array.shape[1] // heads for array in arrays]
    step_rows = max(tok // STEPS, 16)
    wide = sum(widths) // parts

    def kernel(*refs):
        outs = refs[len(arrays) :]
        for index, width in enumerate(widths):
            left = sum(widths[:index])
            cut = min(width, wide)
            for head in range(n_head):
                for local in range(group):
                    for begin in range(0, width, cut):
                        source = (head * group + local) * width + begin
                        out, at = outs[(left + begin) // wide], (left + begin) % wide
                        out[local * n_head + head, :, at : at + cut] = refs[index][:, source : source + cut]

    return pl.pallas_call(
        kernel,
        grid=(tok // step_rows,),
        in_specs=[pl.BlockSpec((step_rows, array.shape[1]), lambda i: (i, 0)) for array in arrays],
        out_specs=[pl.BlockSpec((heads, step_rows, wide), lambda i: (0, i, 0))] * parts,
        out_shape=[jax.ShapeDtypeStruct((heads, tok, wide), arrays[0].dtype)] * parts,
        compiler_params=pltpu.CompilerParams(vmem_limit_bytes=VMEM_FIRST),
        name=name,
    )(*arrays)


def laid_out(received, planes, group):
    _, rows, features = received[0].shape

    def kernel(*refs):
        out = refs[-1]
        for local in range(group):
            for index, blocks in enumerate(refs[:-1]):
                left = (local * len(received) + index) * features
                out[:, left : left + features] = blocks[local]

    wide = group * len(received) * features
    return pl.pallas_call(
        kernel,
        grid=(planes,),
        in_specs=[pl.BlockSpec((group, rows, features), lambda i: (i, 0, 0))] * len(received),
        out_specs=pl.BlockSpec((rows, wide), lambda i: (i, 0)),
        out_shape=jax.ShapeDtypeStruct((planes * rows, wide), received[0].dtype),
        compiler_params=pltpu.CompilerParams(vmem_limit_bytes=VMEM),
        name="lay_out",
    )(*received)


def solution(mesh):
    n_ctx, n_head = mesh.shape["ctx"], mesh.shape["head"]

    def run(queries, keys, values, doc_lengths, piece_owner):
        group = keys.shape[1] // (HD * n_head)
        planes = n_ctx // group
        grouped = Mesh(mesh.devices.reshape(planes, group, n_head), ("plane", "local", "head"))
        rows = P(("plane", "local", "head"), None)

        def exchanged(split):
            moved = lax.all_to_all(split, ("local", "head"), split_axis=0, concat_axis=0, tiled=True)
            return moved.reshape(-1, split.shape[-1])

        def per_device(queries, keys, values, doc_lengths, piece_owner):
            [paired] = dealt([values, keys], n_head, group, 1, "deal_keys")
            owner = lax.all_gather(piece_owner, "local", axis=0, tiled=True)
            split = dealt([queries], n_head, group, PARTS, "deal_queries")
            own, owner, *split = lax.optimization_barrier((exchanged(paired), owner, *split))
            tokens = own.shape[0]
            reach = (MOST - 1) // tokens + 1
            up = [(plane, plane + 1) for plane in range(planes - 1)]
            steps_back = []
            moving = own
            for _ in range(reach):
                moving = lax.ppermute(moving, "plane", up)
                steps_back.append(moving)
            at = (lax.axis_index("plane") * tokens).astype(jnp.int32)[None]
            piece = tokens // (group * n_ctx)
            received = []
            before = None
            for part in split:
                query_rows = exchanged(part)
                if before is not None:
                    query_rows, before = lax.optimization_barrier((query_rows, before))
                    received.append(delivered(before))
                before = attend(at, doc_lengths, owner, n_ctx, piece, query_rows, own, steps_back)
            received.append(delivered(before))
            return laid_out(received, planes, group)

        def delivered(ordered):
            ordered = ordered.reshape(n_ctx, -1, ordered.shape[-1])
            return lax.all_to_all(ordered, ("plane", "local"), split_axis=0, concat_axis=0, tiled=True)

        return jax.shard_map(
            per_device,
            mesh=grouped,
            in_specs=(rows, rows, rows, P(), P(("plane", "local"), None)),
            out_specs=P(("plane", "local"), "head"),
            check_vma=False,
        )(queries, keys, values, doc_lengths, piece_owner)

    return run
```

```python
import math

import jax
import jax.numpy as jnp
from jax import lax
from jax.experimental import pallas as pl
from jax.experimental.pallas import tpu as pltpu
from jax.sharding import Mesh
from jax.sharding import PartitionSpec as P

HD = 128
MOST = 4096
PARTS = 2
Q_ROWS = 512
CHUNK = 256
K_LONG = 1024
K_SHORT = 256
MASKED = -1e30
SCALE = math.log2(math.e) / math.sqrt(HD)
VMEM = 32 * 1024 * 1024
STEPS = 2
VMEM_FIRST = 60 * 1024 * 1024


def doc_start(place, ends):
    start = jnp.zeros_like(place)
    for end in ends:
        start = jnp.maximum(start, jnp.where(end <= place, end, 0))
    return start


class Block:
    def __init__(self, ends, first_row, base, pairs, qs, top, total):
        self.ends = ends
        self.first_row, self.base, self.window = first_row, base, pairs.shape[0]
        self.pairs, self.qs, self.top, self.total = pairs, qs, top, total
        self.heads = qs.shape[0] // Q_ROWS
        self.first_start = doc_start(first_row, self.ends) - base
        self.last_start = doc_start(first_row + Q_ROWS - 1, self.ends) - base

    def load(self, q_ref):
        for head in range(self.heads):
            scaled = q_ref[:, head * HD : (head + 1) * HD].astype(jnp.float32) * SCALE
            high = scaled.astype(jnp.bfloat16)
            rows = slice(head * Q_ROWS, (head + 1) * Q_ROWS)
            self.qs[rows, :HD] = high
            self.qs[rows, HD:] = (scaled - high.astype(jnp.float32)).astype(jnp.bfloat16)

    def run(self, at, size, masked):
        at = pl.multiple_of(at, K_SHORT)
        values = self.pairs[pl.ds(at, size), :HD]
        keys = self.pairs[pl.ds(at, size), HD:]
        keys = jnp.concatenate([keys, keys], axis=1)
        values = jnp.concatenate([values, jnp.ones_like(values)], axis=1)
        lives = []
        if masked:
            place = self.base + at + lax.broadcasted_iota(jnp.int32, (CHUNK, size), 1)
            for first in range(0, Q_ROWS, CHUNK):
                row = self.first_row + first + lax.broadcasted_iota(jnp.int32, (CHUNK, 1), 0)
                lives.append((place <= row) & (place >= doc_start(row, self.ends)))

        def score(chunk):
            return lax.dot_general(
                self.qs[chunk * CHUNK : (chunk + 1) * CHUNK],
                keys,
                (((1,), (1,)), ((), ())),
                preferred_element_type=jnp.float32,
            )

        chunks = self.heads * Q_ROWS // CHUNK
        scores = score(0)
        for chunk in range(chunks):
            rows = slice(chunk * CHUNK, (chunk + 1) * CHUNK)
            upcoming = score(chunk + 1) if chunk + 1 < chunks else None
            if masked:
                scores = jnp.where(lives[chunk % (Q_ROWS // CHUNK)], scores, MASKED)
            old_top = self.top[rows]
            new_top = jnp.maximum(old_top, jnp.max(scores, axis=1, keepdims=True))
            weights = jnp.exp2(scores - jnp.concatenate([new_top] * (size // HD), axis=1))
            part = jnp.dot(weights.astype(jnp.bfloat16), values, preferred_element_type=jnp.float32)
            factor = jnp.exp2(old_top - new_top)
            self.total[rows] = self.total[rows] * jnp.concatenate([factor, factor], axis=1) + part
            self.top[rows] = new_top
            scores = upcoming

    def cover(self, high, long):
        low = jnp.clip(self.first_start, 0, self.window) // K_SHORT * K_SHORT
        plain = (jnp.clip(self.last_start, 0, self.window) + K_SHORT - 1) // K_SHORT * K_SHORT
        middle = max(long // 2, K_SHORT)
        for size, masked, until in ((long, False, plain), (long, True, low), (middle, True, low), (K_SHORT, True, low)):
            count = jnp.maximum(high - until, 0) // size
            lax.fori_loop(
                0,
                count,
                lambda step, _, high=high, size=size, masked=masked: self.run(high - (step + 1) * size, size, masked),
                None,
            )
            high = high - count * size

    def deliver(self, step, owner, stage, out, sems):
        piece = stage.shape[1]
        slots = Q_ROWS // piece
        for head in range(self.heads):
            rows = slice(head * Q_ROWS, (head + 1) * Q_ROWS)
            done = (self.total[rows, :HD] / self.total[rows, HD:]).astype(jnp.bfloat16)
            for part in range(slots):
                stage[step * slots + part, :, head * HD : (head + 1) * HD] = done[part * piece : (part + 1) * piece]
        lax.fori_loop(0, slots, lambda part, _: sent(step * slots + part, owner, stage, out, sems).start(), None)


def sent(slot, owner, stage, out, sems):
    return pltpu.make_async_copy(stage.at[slot], out.at[owner[slot // out.shape[0], slot % out.shape[0]], slot // out.shape[0]], sems.at[slot])


def keep(step, slot, top, total, tops, totals, kept, back):
    pairs = ((top.at[slot], tops.at[step]), (total.at[slot], totals.at[step]))
    if back:
        pairs = [pair[::-1] for pair in pairs]
    return [pltpu.make_async_copy(*pair, kept.at[slot, index]) for index, pair in enumerate(pairs)]


def far_blocks(place, ends, tokens):
    count = 0
    for step in range(tokens // Q_ROWS):
        count += (doc_start(place + step * Q_ROWS, ends) < place - tokens).astype(jnp.int32)
    return count


def ends_of(lengths):
    ends = [lengths[0]]
    for doc in range(1, lengths.shape[0]):
        ends.append(ends[-1] + lengths[doc])
    return ends


def near_kernel(at, lengths, owner, q_ref, own, near, out, tops, totals, pairs, qs, top, total, stage, sems, kept, brought):
    tokens = own.shape[0]
    step = pl.program_id(0)
    slot = lax.rem(step, 2)
    place = at[0]
    ends = ends_of(lengths)
    needed = far_blocks(place, ends, tokens)
    slots = Q_ROWS // stage.shape[1]

    @pl.when(step == 0)
    def _():
        copies = [
            pltpu.make_async_copy(ref, pairs.at[index * tokens : (index + 1) * tokens], brought.at[index])
            for index, ref in enumerate((near, own))
        ]
        for copy in copies:
            copy.start()
        for copy in copies:
            copy.wait()

    @pl.when((step >= 2) & (step - 2 < needed))
    def _():
        for copy in keep(step - 2, slot, top, total, tops, totals, kept, False):
            copy.wait()

    first_row = place + step * Q_ROWS
    block = Block(ends, first_row, place - tokens, pairs, qs, top.at[slot], total.at[slot])
    block.load(q_ref)
    top[slot] = jnp.full(top.shape[1:], MASKED, jnp.float32)
    total[slot] = jnp.zeros(total.shape[1:], jnp.float32)
    long = min(K_LONG, tokens)
    high = tokens + (step + 1) * Q_ROWS - long
    block.run(high, long, True)
    block.cover(high, long)

    @pl.when(step >= needed)
    def _():
        block.deliver(step, owner, stage, out, sems)

    @pl.when(step < needed)
    def _():
        for copy in keep(step, slot, top, total, tops, totals, kept, False):
            copy.start()

    blocks = tokens // Q_ROWS

    @pl.when(step == blocks - 1)
    def _():
        for last in range(max(blocks - 2, 0), blocks):

            @pl.when(last < needed)
            def _(last=last):
                for copy in keep(last, last % 2, top, total, tops, totals, kept, False):
                    copy.wait()

        finish(needed * slots, blocks * slots, owner, stage, out, sems)


def finish(first, last, owner, stage, out, sems):
    lax.fori_loop(first, last, lambda slot, _: sent(slot, owner, stage, out, sems).wait(), None)


def far_kernel(at, lengths, owner, q_rows, tops, totals, begun, *refs):
    far, (out, held, pairs, qs, top, total, stage, sems, kept, brought) = refs[:-10], refs[-10:]
    del begun
    tokens = q_rows.shape[0]
    window = tokens * len(far)
    place = at[0]
    ends = ends_of(lengths)
    needed = far_blocks(place, ends, tokens)

    def coming(step, slot):
        copies = keep(step, slot, top, total, tops, totals, kept, True)
        rows = pl.ds(pl.multiple_of(step * Q_ROWS, Q_ROWS), Q_ROWS)
        return copies + [pltpu.make_async_copy(q_rows.at[rows], held.at[slot], kept.at[slot, 2])]

    @pl.when(needed > 0)
    def _():
        whole = [
            pltpu.make_async_copy(ref, pairs.at[index * tokens : (index + 1) * tokens], brought.at[index])
            for index, ref in enumerate(far[::-1])
        ]
        for copy in whole + coming(0, 0):
            copy.start()
        for copy in whole:
            copy.wait()

    def one(step, carry):
        slot = lax.rem(step, 2)

        @pl.when(step + 1 < needed)
        def _():
            for copy in coming(step + 1, 1 - slot):
                copy.start()

        first_row = place + step * Q_ROWS
        block = Block(ends, first_row, place - tokens - window, pairs, qs, top.at[slot], total.at[slot])
        for copy in coming(step, slot):
            copy.wait()
        block.load(held.at[slot])
        block.cover(window, min(K_LONG, tokens))
        block.deliver(step, owner, stage, out, sems)
        return carry

    lax.fori_loop(0, needed, one, 0)
    finish(0, needed * (Q_ROWS // stage.shape[1]), owner, stage, out, sems)


def attend(at, lengths, owner, n_owner, piece, query_rows, own, steps_back):
    tokens, features = query_rows.shape
    blocks = tokens // Q_ROWS
    near, far = steps_back[0], steps_back[1:]
    rows = features // HD * Q_ROWS
    any_spec = pl.BlockSpec(memory_space=pl.ANY)
    out_shape = jax.ShapeDtypeStruct((n_owner, tokens // (n_owner * piece), piece, features), jnp.bfloat16)
    state_shapes = [
        jax.ShapeDtypeStruct((blocks, rows, HD), jnp.float32),
        jax.ShapeDtypeStruct((blocks, rows, 2 * HD), jnp.float32),
    ]

    def scratch(window):
        return [
            pltpu.VMEM((window, 2 * HD), jnp.bfloat16),
            pltpu.VMEM((rows, 2 * HD), jnp.bfloat16),
            pltpu.VMEM((2, rows, HD), jnp.float32),
            pltpu.VMEM((2, rows, 2 * HD), jnp.float32),
            pltpu.VMEM((tokens // piece, piece, features), jnp.bfloat16),
            pltpu.SemaphoreType.DMA((tokens // piece,)),
            pltpu.SemaphoreType.DMA((2, 3)),
            pltpu.SemaphoreType.DMA((window // tokens,)),
        ]

    begun, tops, totals = pl.pallas_call(
        near_kernel,
        grid_spec=pltpu.PrefetchScalarGridSpec(
            num_scalar_prefetch=3,
            grid=(blocks,),
            in_specs=[pl.BlockSpec((Q_ROWS, features), lambda i, *_: (i, 0)), any_spec, any_spec],
            out_specs=[any_spec] * 3,
            scratch_shapes=scratch(2 * tokens),
        ),
        out_shape=[out_shape, *state_shapes],
        compiler_params=pltpu.CompilerParams(vmem_limit_bytes=VMEM_FIRST),
        cost_estimate=pl.CostEstimate(flops=20_000_000_000, bytes_accessed=1 << 23, transcendentals=0),
        name="attend_near",
    )(at, lengths, owner, query_rows, own, near)
    if not far:
        return begun
    return pl.pallas_call(
        far_kernel,
        grid_spec=pltpu.PrefetchScalarGridSpec(
            num_scalar_prefetch=3,
            grid=(),
            in_specs=[any_spec] * (4 + len(far)),
            out_specs=any_spec,
            scratch_shapes=[
                pltpu.VMEM((2, Q_ROWS, features), jnp.bfloat16),
                *scratch(tokens * len(far)),
            ],
        ),
        out_shape=out_shape,
        input_output_aliases={6: 0},
        compiler_params=pltpu.CompilerParams(vmem_limit_bytes=VMEM_FIRST),
        cost_estimate=pl.CostEstimate(flops=5_000_000_000, bytes_accessed=1 << 23, transcendentals=0),
        name="attend_far",
    )(at, lengths, owner, query_rows, tops, totals, begun, *far)


def dealt(arrays, n_head, group, parts, name):
    heads = n_head * group
    tok = arrays[0].shape[0]
    widths = [array.shape[1] // heads for array in arrays]
    step_rows = max(tok // STEPS, 16)
    wide = sum(widths) // parts

    def kernel(*refs):
        outs = refs[len(arrays) :]
        for index, width in enumerate(widths):
            left = sum(widths[:index])
            cut = min(width, wide)
            for head in range(n_head):
                for local in range(group):
                    for begin in range(0, width, cut):
                        source = (head * group + local) * width + begin
                        out, at = outs[(left + begin) // wide], (left + begin) % wide
                        out[local * n_head + head, :, at : at + cut] = refs[index][:, source : source + cut]

    return pl.pallas_call(
        kernel,
        grid=(tok // step_rows,),
        in_specs=[pl.BlockSpec((step_rows, array.shape[1]), lambda i: (i, 0)) for array in arrays],
        out_specs=[pl.BlockSpec((heads, step_rows, wide), lambda i: (0, i, 0))] * parts,
        out_shape=[jax.ShapeDtypeStruct((heads, tok, wide), arrays[0].dtype)] * parts,
        compiler_params=pltpu.CompilerParams(vmem_limit_bytes=VMEM_FIRST),
        name=name,
    )(*arrays)


def laid_out(received, planes, group):
    _, rows, features = received[0].shape

    def kernel(*refs):
        out = refs[-1]
        for local in range(group):
            for index, blocks in enumerate(refs[:-1]):
                left = (local * len(received) + index) * features
                out[:, left : left + features] = blocks[local]

    wide = group * len(received) * features
    return pl.pallas_call(
        kernel,
        grid=(planes,),
        in_specs=[pl.BlockSpec((group, rows, features), lambda i: (i, 0, 0))] * len(received),
        out_specs=pl.BlockSpec((rows, wide), lambda i: (i, 0)),
        out_shape=jax.ShapeDtypeStruct((planes * rows, wide), received[0].dtype),
        compiler_params=pltpu.CompilerParams(vmem_limit_bytes=VMEM),
        name="lay_out",
    )(*received)


def solution(mesh):
    n_ctx, n_head = mesh.shape["ctx"], mesh.shape["head"]

    def run(queries, keys, values, doc_lengths, piece_owner):
        group = keys.shape[1] // (HD * n_head)
        planes = n_ctx // group
        grouped = Mesh(mesh.devices.reshape(planes, group, n_head), ("plane", "local", "head"))
        rows = P(("plane", "local", "head"), None)

        def exchanged(split):
            moved = lax.all_to_all(split, ("local", "head"), split_axis=0, concat_axis=0, tiled=True)
            return moved.reshape(-1, split.shape[-1])

        def per_device(queries, keys, values, doc_lengths, piece_owner):
            [paired] = dealt([values, keys], n_head, group, 1, "deal_keys")
            owner = lax.all_gather(piece_owner, "local", axis=0, tiled=True)
            split = dealt([queries], n_head, group, PARTS, "deal_queries")
            own, owner, *split = lax.optimization_barrier((exchanged(paired), owner, *split))
            tokens = own.shape[0]
            reach = (MOST - 1) // tokens + 1
            up = [(plane, plane + 1) for plane in range(planes - 1)]
            split[0] = exchanged(split[0])
            moving = lax.ppermute(own, "plane", up)
            split[0], moving = lax.optimization_barrier((split[0], moving))
            steps_back = [moving]
            for _ in range(1, reach):
                moving = lax.ppermute(moving, "plane", up)
                steps_back.append(moving)
            split[1:] = [exchanged(part) for part in split[1:]]
            at = (lax.axis_index("plane") * tokens).astype(jnp.int32)[None]
            piece = tokens // (group * n_ctx)
            received = []
            before = None
            for query_rows in split:
                if before is not None:
                    query_rows, before = lax.optimization_barrier((query_rows, before))
                    received.append(delivered(before))
                before = attend(at, doc_lengths, owner, n_ctx, piece, query_rows, own, steps_back)
            received.append(delivered(before))
            return laid_out(received, planes, group)

        def delivered(ordered):
            ordered = ordered.reshape(n_ctx, -1, ordered.shape[-1])
            return lax.all_to_all(ordered, ("plane", "local"), split_axis=0, concat_axis=0, tiled=True)

        return jax.shard_map(
            per_device,
            mesh=grouped,
            in_specs=(rows, rows, rows, P(), P(("plane", "local"), None)),
            out_specs=P(("plane", "local"), "head"),
            check_vma=False,
        )(queries, keys, values, doc_lengths, piece_owner)

    return run
```

```python
import math

import jax
import jax.numpy as jnp
from jax import lax
from jax.experimental import pallas as pl
from jax.experimental.pallas import tpu as pltpu
from jax.sharding import Mesh
from jax.sharding import PartitionSpec as P

HD = 128
MOST = 4096
PARTS = 2
Q_ROWS = 512
CHUNK = 256
K_LONG = 1024
K_SHORT = 256
MASKED = -1e30
SCALE = math.log2(math.e) / math.sqrt(HD)
VMEM = 32 * 1024 * 1024
STEPS = 2
VMEM_FIRST = 60 * 1024 * 1024


def halved(number, power):
    return lax.shift_right_logical(number, jnp.int32(power.bit_length() - 1))


def doc_start(place, ends):
    start = jnp.zeros_like(place)
    for end in ends:
        start = jnp.maximum(start, jnp.where(end <= place, end, 0))
    return start


class Block:
    def __init__(self, ends, first_row, base, pairs, qs, top, total):
        self.ends = ends
        self.first_row, self.base, self.window = first_row, base, pairs.shape[0]
        self.pairs, self.qs, self.top, self.total = pairs, qs, top, total
        self.heads = qs.shape[0] // Q_ROWS
        self.first_start = doc_start(first_row, self.ends) - base
        self.last_start = doc_start(first_row + Q_ROWS - 1, self.ends) - base

    def load(self, q_ref):
        for head in range(self.heads):
            scaled = q_ref[:, head * HD : (head + 1) * HD].astype(jnp.float32) * SCALE
            high = scaled.astype(jnp.bfloat16)
            rows = slice(head * Q_ROWS, (head + 1) * Q_ROWS)
            self.qs[rows, :HD] = high
            self.qs[rows, HD:] = (scaled - high.astype(jnp.float32)).astype(jnp.bfloat16)

    def run(self, at, size, masked):
        at = pl.multiple_of(at, K_SHORT)
        width = min(size, K_LONG)
        chunks = self.heads * Q_ROWS // CHUNK
        work = [(left, chunk) for left in range(0, size, width) for chunk in range(chunks)]
        lives = []
        if masked:
            place = self.base + at + lax.broadcasted_iota(jnp.int32, (CHUNK, size), 1)
            for first in range(0, Q_ROWS, CHUNK):
                row = self.first_row + first + lax.broadcasted_iota(jnp.int32, (CHUNK, 1), 0)
                lives.append((place <= row) & (place >= doc_start(row, self.ends)))

        def score(left, chunk):
            keys = self.pairs[pl.ds(at + left, width), HD:]
            return lax.dot_general(
                self.qs[chunk * CHUNK : (chunk + 1) * CHUNK],
                jnp.concatenate([keys, keys], axis=1),
                (((1,), (1,)), ((), ())),
                preferred_element_type=jnp.float32,
            )

        scores = score(*work[0])
        for number, (left, chunk) in enumerate(work):
            rows = slice(chunk * CHUNK, (chunk + 1) * CHUNK)
            upcoming = score(*work[number + 1]) if number + 1 < len(work) else None
            if masked:
                scores = jnp.where(lives[chunk % (Q_ROWS // CHUNK)], scores, MASKED)
            values = self.pairs[pl.ds(at + left, width), :HD]
            values = jnp.concatenate([values, jnp.ones_like(values)], axis=1)
            old_top = self.top[rows]
            new_top = jnp.maximum(old_top, jnp.max(scores, axis=1, keepdims=True))
            weights = jnp.exp2(scores - jnp.concatenate([new_top] * (width // HD), axis=1))
            part = jnp.dot(weights.astype(jnp.bfloat16), values, preferred_element_type=jnp.float32)
            factor = jnp.exp2(old_top - new_top)
            self.total[rows] = self.total[rows] * jnp.concatenate([factor, factor], axis=1) + part
            self.top[rows] = new_top
            scores = upcoming

    def cover(self, high, long):
        low = jnp.clip(self.first_start, 0, self.window) & -K_SHORT
        plain = (jnp.clip(self.last_start, 0, self.window) + (K_SHORT - 1)) & -K_SHORT
        middle = max(long // 2, K_SHORT)
        shapes = (
            (2 * long, False, plain),
            (long, False, plain),
            (middle, False, plain),
            (long, True, low),
            (middle, True, low),
            (K_SHORT, True, low),
        )
        for size, masked, until in shapes:
            count = halved(jnp.maximum(high - until, 0), size)
            lax.fori_loop(
                0,
                count,
                lambda step, _, high=high, size=size, masked=masked: self.run(high - (step + 1) * size, size, masked),
                None,
            )
            high = high - count * size

    def deliver(self, step, owner, stage, out, sems):
        piece = stage.shape[1]
        slots = Q_ROWS // piece
        for head in range(self.heads):
            rows = slice(head * Q_ROWS, (head + 1) * Q_ROWS)
            done = (self.total[rows, :HD] / self.total[rows, HD:]).astype(jnp.bfloat16)
            for part in range(slots):
                stage[step * slots + part, :, head * HD : (head + 1) * HD] = done[part * piece : (part + 1) * piece]
        lax.fori_loop(0, slots, lambda part, _: sent(step * slots + part, owner, stage, out, sems).start(), None)


def sent(slot, owner, stage, out, sems):
    n_owner = out.shape[0]
    shard = halved(slot, n_owner)
    return pltpu.make_async_copy(stage.at[slot], out.at[owner[shard, slot & (n_owner - 1)], shard], sems.at[slot])


def keep(step, slot, top, total, tops, totals, kept, back):
    pairs = ((top.at[slot], tops.at[step]), (total.at[slot], totals.at[step]))
    if back:
        pairs = [pair[::-1] for pair in pairs]
    return [pltpu.make_async_copy(*pair, kept.at[slot, index]) for index, pair in enumerate(pairs)]


def far_blocks(place, ends, tokens):
    count = 0
    for step in range(tokens // Q_ROWS):
        count += (doc_start(place + step * Q_ROWS, ends) < place - tokens).astype(jnp.int32)
    return count


def ends_of(lengths):
    ends = [lengths[0]]
    for doc in range(1, lengths.shape[0]):
        ends.append(ends[-1] + lengths[doc])
    return ends


def near_kernel(at, lengths, owner, q_ref, own, near, out, tops, totals, pairs, qs, top, total, stage, sems, kept, brought):
    tokens = own.shape[0]
    step = pl.program_id(0)
    slot = step & 1
    place = at[0]
    ends = ends_of(lengths)
    needed = far_blocks(place, ends, tokens)
    slots = Q_ROWS // stage.shape[1]

    @pl.when(step == 0)
    def _():
        copies = [
            pltpu.make_async_copy(ref, pairs.at[index * tokens : (index + 1) * tokens], brought.at[index])
            for index, ref in enumerate((near, own))
        ]
        for copy in copies:
            copy.start()
        for copy in copies:
            copy.wait()

    @pl.when((step >= 2) & (step - 2 < needed))
    def _():
        for copy in keep(step - 2, slot, top, total, tops, totals, kept, False):
            copy.wait()

    first_row = place + step * Q_ROWS
    block = Block(ends, first_row, place - tokens, pairs, qs, top.at[slot], total.at[slot])
    block.load(q_ref)
    top[slot] = jnp.full(top.shape[1:], MASKED, jnp.float32)
    total[slot] = jnp.zeros(total.shape[1:], jnp.float32)
    long = min(K_LONG, tokens)
    high = tokens + step * Q_ROWS
    block.run(high, Q_ROWS, True)
    block.cover(high, long)

    @pl.when(step >= needed)
    def _():
        block.deliver(step, owner, stage, out, sems)

    @pl.when(step < needed)
    def _():
        for copy in keep(step, slot, top, total, tops, totals, kept, False):
            copy.start()

    blocks = tokens // Q_ROWS

    @pl.when(step == blocks - 1)
    def _():
        for last in range(max(blocks - 2, 0), blocks):

            @pl.when(last < needed)
            def _(last=last):
                for copy in keep(last, last % 2, top, total, tops, totals, kept, False):
                    copy.wait()

        finish(needed * slots, blocks * slots, owner, stage, out, sems)


def finish(first, last, owner, stage, out, sems):
    lax.fori_loop(first, last, lambda slot, _: sent(slot, owner, stage, out, sems).wait(), None)


def far_kernel(at, lengths, owner, q_rows, tops, totals, begun, *refs):
    far, (out, held, pairs, qs, top, total, stage, sems, kept, brought) = refs[:-10], refs[-10:]
    del begun
    tokens = q_rows.shape[0]
    window = tokens * len(far)
    place = at[0]
    ends = ends_of(lengths)
    needed = far_blocks(place, ends, tokens)

    def coming(step, slot):
        copies = keep(step, slot, top, total, tops, totals, kept, True)
        rows = pl.ds(pl.multiple_of(step * Q_ROWS, Q_ROWS), Q_ROWS)
        return copies + [pltpu.make_async_copy(q_rows.at[rows], held.at[slot], kept.at[slot, 2])]

    @pl.when(needed > 0)
    def _():
        whole = [
            pltpu.make_async_copy(ref, pairs.at[index * tokens : (index + 1) * tokens], brought.at[index])
            for index, ref in enumerate(far[::-1])
        ]
        for copy in whole + coming(0, 0):
            copy.start()
        for copy in whole:
            copy.wait()

    def one(step, carry):
        slot = step & 1

        @pl.when(step + 1 < needed)
        def _():
            for copy in coming(step + 1, 1 - slot):
                copy.start()

        first_row = place + step * Q_ROWS
        block = Block(ends, first_row, place - tokens - window, pairs, qs, top.at[slot], total.at[slot])
        for copy in coming(step, slot):
            copy.wait()
        block.load(held.at[slot])
        block.cover(window, min(K_LONG, tokens))
        block.deliver(step, owner, stage, out, sems)
        return carry

    lax.fori_loop(0, needed, one, 0)
    finish(0, needed * (Q_ROWS // stage.shape[1]), owner, stage, out, sems)


def attend(at, lengths, owner, n_owner, piece, query_rows, own, steps_back):
    tokens, features = query_rows.shape
    blocks = tokens // Q_ROWS
    near, far = steps_back[0], steps_back[1:]
    rows = features // HD * Q_ROWS
    any_spec = pl.BlockSpec(memory_space=pl.ANY)
    out_shape = jax.ShapeDtypeStruct((n_owner, tokens // (n_owner * piece), piece, features), jnp.bfloat16)
    state_shapes = [
        jax.ShapeDtypeStruct((blocks, rows, HD), jnp.float32),
        jax.ShapeDtypeStruct((blocks, rows, 2 * HD), jnp.float32),
    ]

    def scratch(window):
        return [
            pltpu.VMEM((window, 2 * HD), jnp.bfloat16),
            pltpu.VMEM((rows, 2 * HD), jnp.bfloat16),
            pltpu.VMEM((2, rows, HD), jnp.float32),
            pltpu.VMEM((2, rows, 2 * HD), jnp.float32),
            pltpu.VMEM((tokens // piece, piece, features), jnp.bfloat16),
            pltpu.SemaphoreType.DMA((tokens // piece,)),
            pltpu.SemaphoreType.DMA((2, 3)),
            pltpu.SemaphoreType.DMA((window // tokens,)),
        ]

    begun, tops, totals = pl.pallas_call(
        near_kernel,
        grid_spec=pltpu.PrefetchScalarGridSpec(
            num_scalar_prefetch=3,
            grid=(blocks,),
            in_specs=[pl.BlockSpec((Q_ROWS, features), lambda i, *_: (i, 0)), any_spec, any_spec],
            out_specs=[any_spec] * 3,
            scratch_shapes=scratch(2 * tokens),
        ),
        out_shape=[out_shape, *state_shapes],
        compiler_params=pltpu.CompilerParams(vmem_limit_bytes=VMEM_FIRST),
        cost_estimate=pl.CostEstimate(flops=20_000_000_000, bytes_accessed=1 << 23, transcendentals=0),
        name="attend_near",
    )(at, lengths, owner, query_rows, own, near)
    if not far:
        return begun
    return pl.pallas_call(
        far_kernel,
        grid_spec=pltpu.PrefetchScalarGridSpec(
            num_scalar_prefetch=3,
            grid=(),
            in_specs=[any_spec] * (4 + len(far)),
            out_specs=any_spec,
            scratch_shapes=[
                pltpu.VMEM((2, Q_ROWS, features), jnp.bfloat16),
                *scratch(tokens * len(far)),
            ],
        ),
        out_shape=out_shape,
        input_output_aliases={6: 0},
        compiler_params=pltpu.CompilerParams(vmem_limit_bytes=VMEM_FIRST),
        cost_estimate=pl.CostEstimate(flops=5_000_000_000, bytes_accessed=1 << 23, transcendentals=0),
        name="attend_far",
    )(at, lengths, owner, query_rows, tops, totals, begun, *far)


def dealt(arrays, n_head, group, parts, name):
    heads = n_head * group
    tok = arrays[0].shape[0]
    widths = [array.shape[1] // heads for array in arrays]
    step_rows = max(tok // STEPS, 16)
    wide = sum(widths) // parts

    def kernel(*refs):
        outs = refs[len(arrays) :]
        for index, width in enumerate(widths):
            left = sum(widths[:index])
            cut = min(width, wide)
            for head in range(n_head):
                for local in range(group):
                    for begin in range(0, width, cut):
                        source = (head * group + local) * width + begin
                        out, at = outs[(left + begin) // wide], (left + begin) % wide
                        out[local * n_head + head, :, at : at + cut] = refs[index][:, source : source + cut]

    return pl.pallas_call(
        kernel,
        grid=(tok // step_rows,),
        in_specs=[pl.BlockSpec((step_rows, array.shape[1]), lambda i: (i, 0)) for array in arrays],
        out_specs=[pl.BlockSpec((heads, step_rows, wide), lambda i: (0, i, 0))] * parts,
        out_shape=[jax.ShapeDtypeStruct((heads, tok, wide), arrays[0].dtype)] * parts,
        compiler_params=pltpu.CompilerParams(vmem_limit_bytes=VMEM_FIRST),
        name=name,
    )(*arrays)


def laid_out(received, planes, group):
    _, rows, features = received[0].shape

    def kernel(*refs):
        out = refs[-1]
        for local in range(group):
            for index, blocks in enumerate(refs[:-1]):
                left = (local * len(received) + index) * features
                out[:, left : left + features] = blocks[local]

    wide = group * len(received) * features
    return pl.pallas_call(
        kernel,
        grid=(planes,),
        in_specs=[pl.BlockSpec((group, rows, features), lambda i: (i, 0, 0))] * len(received),
        out_specs=pl.BlockSpec((rows, wide), lambda i: (i, 0)),
        out_shape=jax.ShapeDtypeStruct((planes * rows, wide), received[0].dtype),
        compiler_params=pltpu.CompilerParams(vmem_limit_bytes=VMEM),
        name="lay_out",
    )(*received)


def solution(mesh):
    n_ctx, n_head = mesh.shape["ctx"], mesh.shape["head"]

    def run(queries, keys, values, doc_lengths, piece_owner):
        group = keys.shape[1] // (HD * n_head)
        planes = n_ctx // group
        grouped = Mesh(mesh.devices.reshape(planes, group, n_head), ("plane", "local", "head"))
        rows = P(("plane", "local", "head"), None)

        def exchanged(split):
            moved = lax.all_to_all(split, ("local", "head"), split_axis=0, concat_axis=0, tiled=True)
            return moved.reshape(-1, split.shape[-1])

        def per_device(queries, keys, values, doc_lengths, piece_owner):
            [paired] = dealt([values, keys], n_head, group, 1, "deal_keys")
            owner = lax.all_gather(piece_owner, "local", axis=0, tiled=True)
            split = dealt([queries], n_head, group, PARTS, "deal_queries")
            own, owner, *split = lax.optimization_barrier((exchanged(paired), owner, *split))
            tokens = own.shape[0]
            reach = (MOST - 1) // tokens + 1
            up = [(plane, plane + 1) for plane in range(planes - 1)]
            split[0] = exchanged(split[0])
            moving = lax.ppermute(own, "plane", up)
            split[0], moving = lax.optimization_barrier((split[0], moving))
            steps_back = [moving]
            for _ in range(1, reach):
                moving = lax.ppermute(moving, "plane", up)
                steps_back.append(moving)
            split[1:] = [exchanged(part) for part in split[1:]]
            at = (lax.axis_index("plane") * tokens).astype(jnp.int32)[None]
            piece = tokens // (group * n_ctx)
            received = []
            before = None
            for query_rows in split:
                if before is not None:
                    query_rows, before = lax.optimization_barrier((query_rows, before))
                    received.append(delivered(before))
                before = attend(at, doc_lengths, owner, n_ctx, piece, query_rows, own, steps_back)
            received.append(delivered(before))
            return laid_out(received, planes, group)

        def delivered(ordered):
            ordered = ordered.reshape(n_ctx, -1, ordered.shape[-1])
            return lax.all_to_all(ordered, ("plane", "local"), split_axis=0, concat_axis=0, tiled=True)

        return jax.shard_map(
            per_device,
            mesh=grouped,
            in_specs=(rows, rows, rows, P(), P(("plane", "local"), None)),
            out_specs=P(("plane", "local"), "head"),
            check_vma=False,
        )(queries, keys, values, doc_lengths, piece_owner)

    return run
```
